256 devices in a mesh: gs: 64 (over y, z, core), view: 4 (over x).
Axes of the slice: x: 4, y: 4, z: 8, core: 2. Of those that a mesh axis runs over, the one named last changes fastest.
Arguments:
- gauss_params: float32 [59, 524288], P(None, 'gs'), may hold values from -104 to 104
- first_moment: float32 [59, 524288], P(None, 'gs'), may hold values from -4 to 4
- second_moment: float32 [59, 524288], P(None, 'gs'), may hold values from 0.001 to 1
- view_pose: float32 [4, 4], P('view'), may hold values from -259 to 3
- tile_blocks: int32 [4, 512, 16], P('view', 'gs'), may hold values from -1 to 4095, as said below
- tile_order: int32 [4, 512, 16], P('view', 'gs'), may hold values from 0 to 15, as said below
- target_image: float32 [4, 512, 3, 256], P('view', 'gs'), may hold values from 0 to 1
Outputs:
- new_params: float32 [59, 524288], P(None, 'gs')
- new_first: float32 [59, 524288], P(None, 'gs')
- new_second: float32 [59, 524288], P(None, 'gs')
- rendered: float32 [4, 512, 3, 256], P('view', 'gs')
The draws below stay inside these ranges and needn't reach their ends.
Inputs may be any that keep to these rules, and one draw needn't show every extreme that they name: `tile_blocks`: block b is held by index b // 64 of gs. In each view, the lists of the 8 tiles of one index of gs name at most 2 blocks held by one index of gs, and some reach 2; no block is named twice in them. tile_order[v, t] is a permutation of the 16 slots.
All inputs are finite; a program needn't handle non-finite values.
Results may differ from the reference program's by a relative error of at most 0.0003.
Values sent between devices are 32-bit elements; how exact they have to be, the bound alone decides.
No kernel may reach another device: no remote copies, remote signals or barrier semaphores. Data moves between devices by JAX's collectives and lax.ppermute only.
A program may use at most 128 MiB of HBM per device.

```python
import math
import jax
import jax.numpy as jnp
from jax import lax

PARAMS = 59
BLK = 128
KMAX = 16
TILE_PIX = 256
ADAM_STEP = 20
TILES_DEV = 8
BLK_DEV = 64
GAUSS = 524288
CAP = 2
SHIFT_MOST = 16
VIEWS = 4
TILES = 512
N_GS = 64


def scene_layout(key):
    row_slots = TILES_DEV * KMAX
    per_row = row_slots // CAP
    scene_rows = N_GS + SHIFT_MOST
    key_shift, key_owner, key_rank, key_layer = jax.random.split(key, 4)
    shifts = jax.random.randint(key_shift, (VIEWS,), 0, SHIFT_MOST + 1)
    scores = jax.random.randint(key_owner, (scene_rows, row_slots), 0, 1 << 20) * row_slots + jnp.arange(row_slots, dtype=jnp.int32)[None, :]
    placed = jnp.argsort(scores, axis=1).astype(jnp.int32)
    holder = (jnp.arange(scene_rows, dtype=jnp.int32)[:, None] * per_row + placed // CAP) % N_GS
    slots_all = scene_rows * row_slots
    mixing = jax.random.permutation(key_rank, slots_all).astype(jnp.int32)
    ordering = jnp.argsort(holder.reshape(-1) * slots_all + mixing).astype(jnp.int32)
    per_holder = slots_all // N_GS
    position = jnp.zeros((slots_all,), jnp.int32).at[ordering].set(jnp.arange(slots_all, dtype=jnp.int32) % per_holder)
    block_grid = jnp.where(position < BLK_DEV, holder.reshape(-1) * BLK_DEV + position, -1).reshape(scene_rows, row_slots)
    layer_scores = jax.random.randint(key_layer, (scene_rows, TILES_DEV, KMAX), 0, 1 << 20) * KMAX + jnp.arange(KMAX, dtype=jnp.int32)
    layers = jnp.argsort(layer_scores, axis=2).astype(jnp.int32)
    home_slot = ordering.reshape(N_GS, per_holder)[:, :BLK_DEV].reshape(-1)
    return (shifts, block_grid, layers, home_slot)


def base_angles(key):
    key_yaw, key_tilt, key_signs = jax.random.split(jax.random.fold_in(key, 11), 3)
    yaw_size = jax.random.uniform(key_yaw, (), minval=0.4, maxval=1.2)
    tilt_size = jax.random.uniform(key_tilt, (), minval=0.3, maxval=0.6)
    signs = (2 * jax.random.randint(key_signs, (2,), 0, 2) - 1).astype(jnp.float32)
    return (signs[0] * yaw_size, signs[1] * tilt_size)


def draw_tile_blocks(key, part):
    shifts, block_grid, layers, home_slot = scene_layout(key)
    view_rows = jnp.arange(N_GS, dtype=jnp.int32)[None, :] + shifts[:, None]
    return block_grid[view_rows].reshape(VIEWS, TILES, KMAX).astype(jnp.int32)


def draw_tile_order(key, part):
    shifts, block_grid, layers, home_slot = scene_layout(key)
    view_rows = jnp.arange(N_GS, dtype=jnp.int32)[None, :] + shifts[:, None]
    return jnp.argsort(layers[view_rows], axis=3).reshape(VIEWS, TILES, KMAX).astype(jnp.int32)


def draw_view_pose(key, part):
    shifts, block_grid, layers, home_slot = scene_layout(key)
    yaw_base, tilt_base = base_angles(key)
    key = jax.random.fold_in(key, 5)
    subkeys = jax.random.split(key, 3)
    yaw_angle = yaw_base + jax.random.uniform(subkeys[0], (VIEWS,), minval=-0.002, maxval=0.002)
    tilt_angle = tilt_base + jax.random.uniform(subkeys[1], (VIEWS,), minval=-0.03, maxval=0.03)
    nudges = jax.random.uniform(subkeys[2], (VIEWS, 2), minval=-3.0, maxval=3.0)
    return jnp.stack([yaw_angle, tilt_angle, nudges[:, 0], nudges[:, 1] - 16.0 * shifts.astype(jnp.float32)], axis=1)


def draw_gauss_params(key, part):
    shifts, block_grid, layers, home_slot = scene_layout(key)
    yaw_base, tilt_base = base_angles(key)
    key = jax.random.fold_in(key, 7)
    subkeys = jax.random.split(key, 5)
    row_slots = TILES_DEV * KMAX
    scene_row = home_slot // row_slots
    slot_in = home_slot % row_slots
    column = slot_in // KMAX
    depth = layers[scene_row, column, slot_in % KMAX]
    columns_all = N_GS * BLK_DEV * BLK
    rank_in = jnp.arange(BLK, dtype=jnp.float32)
    jitter = jax.random.uniform(subkeys[0], (3, N_GS * BLK_DEV, BLK))
    lateral = column.astype(jnp.float32)[:, None] + 0.1 + 0.8 * jitter[0]
    vertical = scene_row.astype(jnp.float32)[:, None] + 0.1 + 0.8 * jitter[1]
    distance = 0.5 * depth.astype(jnp.float32)[:, None] + 0.4 * (rank_in[None, :] + jitter[2]) / BLK
    sin_yaw, cos_yaw = (jnp.sin(yaw_base), jnp.cos(yaw_base))
    sin_tilt, cos_tilt = (jnp.sin(tilt_base), jnp.cos(tilt_base))
    centre_first = lateral * cos_yaw + vertical * sin_yaw * sin_tilt + distance * sin_yaw * cos_tilt
    centre_second = vertical * cos_tilt - distance * sin_tilt
    centre_third = -lateral * sin_yaw + vertical * cos_yaw * sin_tilt + distance * cos_yaw * cos_tilt
    centre = jnp.stack([centre_first, centre_second, centre_third]).reshape(3, columns_all)
    log_scale = jax.random.uniform(subkeys[1], (3, columns_all), minval=-0.5, maxval=0.2)
    quaternion = 0.6 * jax.random.truncated_normal(subkeys[2], -4.0, 4.0, (4, columns_all))
    logits = jax.random.uniform(subkeys[3], (1, columns_all), minval=-12.0, maxval=-4.5)
    harmonic = jax.random.truncated_normal(subkeys[4], -4.0, 4.0, (3, 16, columns_all))
    boosts = jnp.where(jnp.arange(16) == 0, 1.2, 0.2)
    harmonic = (harmonic * boosts[None, :, None]).reshape(48, columns_all)
    return jnp.concatenate([centre, log_scale, quaternion, logits, harmonic], axis=0).astype(jnp.float32)


def block_levels(key, dims, cuts, smallest, top_value):
    loudness, own = 1.0, jax.random.fold_in(key, 6)
    for axis_at, shards_of in cuts:
        steps = jnp.exp(jax.random.uniform(jax.random.fold_in(own, axis_at), (shards_of,), jnp.float32, smallest / len(cuts), top_value / len(cuts)))
        loudness = loudness * jnp.repeat(steps, dims[axis_at] // shards_of).reshape([-1 if axis == axis_at else 1 for axis in range(len(dims))])
    return loudness


def normal_values(rng, dims, scale, reach, cuts=(), kind=jnp.bfloat16):
    entries = jax.random.normal(rng, dims, jnp.float32) * scale
    if len(cuts) > 0:
        entries = block_levels(rng, dims, cuts, -0.22, 0.18) * entries
    return jnp.clip(entries, min=-reach, max=reach).astype(kind)


def setup_inputs(seed: int = 0) -> dict:
    keys = jax.random.split(jax.random.key(seed), 8)
    return {
        "gauss_params": draw_gauss_params(jax.random.fold_in(keys[7], 71), 0),
        "first_moment": normal_values(keys[1], (PARAMS, GAUSS), 0.3, 4.0, ((1, 64),), jnp.float32),
        "second_moment": jnp.clip(jnp.exp(math.log(1.0) - 6.9077552 * jax.random.uniform(keys[2], (PARAMS, GAUSS), jnp.float32) ** block_levels(keys[2], (PARAMS, GAUSS), ((1, 64),), -0.2, 0.2)), 0.001, 1.0),
        "view_pose": draw_view_pose(jax.random.fold_in(keys[7], 71), 0),
        "tile_blocks": draw_tile_blocks(jax.random.fold_in(keys[7], 71), 0),
        "tile_order": draw_tile_order(jax.random.fold_in(keys[7], 71), 0),
        "target_image": jnp.clip(1.0 * jax.random.uniform(keys[6], (VIEWS, TILES, 3, TILE_PIX), jnp.float32) ** block_levels(keys[6], (VIEWS, TILES, 3, TILE_PIX), ((0, 4), (1, 64)), -0.2, 0.2), 0.0, 1.0),
    }


beta_one = 0.9
beta_two = 0.999
learn_rate = 0.01
adam_eps = 1e-08
dilation = 0.3

def harmonics(look_axis):
    x, y, z = (look_axis[0], look_axis[1], look_axis[2])
    square_x, square_y, square_z = (x * x, y * y, z * z)
    return jnp.stack([0.28209479177387814 + 0.0 * x, -0.4886025119029199 * y, 0.4886025119029199 * z, -0.4886025119029199 * x, 1.0925484305920792 * x * y, -1.0925484305920792 * y * z, 0.31539156525252005 * (2.0 * square_z - square_x - square_y), -1.0925484305920792 * x * z, 0.5462742152960396 * (square_x - square_y), -0.5900435899266435 * y * (3.0 * square_x - square_y), 2.890611442640554 * x * y * z, -0.4570457994644658 * y * (4.0 * square_z - square_x - square_y), 0.3731763325901154 * z * (2.0 * square_z - 3.0 * square_x - 3.0 * square_y), -0.4570457994644658 * x * (4.0 * square_z - square_x - square_y), 1.445305721320277 * z * (square_x - square_y), -0.5900435899266435 * x * (square_x - 3.0 * square_y)])

def project(params, camera):
    sin_yaw, cos_yaw = (jnp.sin(camera[0]), jnp.cos(camera[0]))
    sin_tilt, cos_tilt = (jnp.sin(camera[1]), jnp.cos(camera[1]))
    right_axis = (cos_yaw, 0.0 * cos_yaw, -sin_yaw)
    upward = (sin_yaw * sin_tilt, cos_tilt, cos_yaw * sin_tilt)
    look_axis = jnp.stack([sin_yaw * cos_tilt, -sin_tilt, cos_yaw * cos_tilt])
    centre = params[0:3]
    across = 16.0 * (right_axis[0] * centre[0] + right_axis[1] * centre[1] + right_axis[2] * centre[2]) + camera[2]
    downward = 16.0 * (upward[0] * centre[0] + upward[1] * centre[1] + upward[2] * centre[2]) + camera[3]
    scales = jnp.exp(params[3:6])
    quaternion = params[6:10]
    length = lax.optimization_barrier(jnp.sum(quaternion * quaternion, axis=0))
    quaternion = quaternion * lax.rsqrt(jnp.maximum(length, 1.0))
    w, x, y, z = (quaternion[0], quaternion[1], quaternion[2], quaternion[3])
    rotation = ((1.0 - 2.0 * (y * y + z * z), 2.0 * (x * y - w * z), 2.0 * (x * z + w * y)), (2.0 * (x * y + w * z), 1.0 - 2.0 * (x * x + z * z), 2.0 * (y * z - w * x)), (2.0 * (x * z - w * y), 2.0 * (y * z + w * x), 1.0 - 2.0 * (x * x + y * y)))
    mapped = []
    for direction in (right_axis, upward):
        mapped.append([16.0 * scales[k] * (direction[0] * rotation[0][k] + direction[1] * rotation[1][k] + direction[2] * rotation[2][k]) for k in range(3)])
    first_row, second_row = mapped
    spread_first = first_row[0] * first_row[0] + first_row[1] * first_row[1] + first_row[2] * first_row[2] + dilation
    spread_mixed = first_row[0] * second_row[0] + first_row[1] * second_row[1] + first_row[2] * second_row[2]
    spread_second = second_row[0] * second_row[0] + second_row[1] * second_row[1] + second_row[2] * second_row[2] + dilation
    determinant = spread_first * spread_second - spread_mixed * spread_mixed
    opacity = jax.nn.sigmoid(params[10])
    harmonic = harmonics(look_axis).reshape((1, 16) + (1,) * (params.ndim - 1))
    coeffs = params[11:59].reshape((3, 16) + params.shape[1:])
    colour = jnp.maximum(0.5 + lax.optimization_barrier(jnp.sum(harmonic * coeffs, axis=1)), 0.0)
    return jnp.concatenate([jnp.stack([across, downward, spread_second / determinant, -spread_mixed / determinant, spread_first / determinant, opacity]), colour], axis=0)

def composite(ordered, active, across, downward):

    def advance(carry, inputs):
        transmit, colour = carry
        feature, weight_on = inputs
        offset_x = across[None, :] - feature[0][:, None]
        offset_y = downward[None, :] - feature[1][:, None]
        exponent = 0.5 * (feature[2][:, None] * offset_x * offset_x + 2.0 * feature[3][:, None] * offset_x * offset_y + feature[4][:, None] * offset_y * offset_y)
        alphas = weight_on * feature[5][:, None] * jnp.exp(-exponent)
        losses = jnp.log1p(-alphas)
        running = jnp.cumsum(losses, axis=0)
        weights = alphas * transmit[None, :] * jnp.exp(running - losses)
        colour = colour + jnp.dot(feature[6:9], weights, precision=lax.Precision.HIGHEST, preferred_element_type=jnp.float32)
        return ((transmit * jnp.exp(running[-1]), colour), None)
    initial = (jnp.ones(across.shape, jnp.float32), jnp.zeros((3,) + across.shape, jnp.float32))
    (transmit, colour), _ = lax.scan(jax.checkpoint(advance), initial, (ordered, active))
    return colour

def render_row(gathered, in_use, depth_order, row_index, goal_image):
    ordered = jnp.take_along_axis(gathered, depth_order[:, :, None, None], axis=1)
    active = jnp.take_along_axis(in_use, depth_order, axis=1)
    pixels = jnp.arange(TILE_PIX, dtype=jnp.int32)
    tile_col = jnp.arange(gathered.shape[0], dtype=jnp.int32)
    across = (16 * tile_col[:, None] + pixels[None, :] % 16).astype(jnp.float32) + 0.5
    downward = (16 * row_index + pixels // 16).astype(jnp.float32) + 0.5
    downward = jnp.broadcast_to(downward[None, :], across.shape)
    rendered = jax.vmap(composite)(ordered, active, across, downward)
    total_loss = 0.5 * jnp.sum((rendered - goal_image) ** 2)
    return (total_loss, rendered)

def apply_adam(weights_in, moment_one, moment_two, gradient):
    new_first = beta_one * moment_one + (1.0 - beta_one) * gradient
    new_second = beta_two * moment_two + (1.0 - beta_two) * gradient * gradient
    step_size = learn_rate / (1.0 - beta_one ** ADAM_STEP)
    new_params = weights_in - step_size * new_first / (jnp.sqrt(new_second / (1.0 - beta_two ** ADAM_STEP)) + adam_eps)
    return (new_params, new_first, new_second)

def reference(gauss_params, first_moment, second_moment, view_pose, tile_blocks, tile_order, target_image):
    columns = gauss_params.shape[1]
    block_count = columns // BLK
    gradient = jnp.zeros_like(gauss_params)
    images = []
    for v in range(VIEWS):
        camera = view_pose[v]
        features, pullback = jax.vjp(lambda p: project(p, camera), gauss_params)
        lookup = features.reshape(9, block_count, BLK)
        view_blocks = tile_blocks[v]
        view_order = tile_order[v]
        view_goal = target_image[v]

        def one_row(totals, row_index):
            offset = (row_index * TILES_DEV).astype(jnp.int32)
            block_ids = lax.dynamic_slice_in_dim(view_blocks, offset, TILES_DEV, 0)
            depth_order = lax.dynamic_slice_in_dim(view_order, offset, TILES_DEV, 0)
            goal_image = lax.dynamic_slice_in_dim(view_goal, offset, TILES_DEV, 0)
            in_use = (block_ids >= 0).astype(jnp.float32)
            safe_ids = jnp.maximum(block_ids, 0).reshape(-1)
            gathered = jnp.take(lookup, safe_ids, axis=1).reshape(9, TILES_DEV, KMAX, BLK)
            gathered = jnp.transpose(gathered, (1, 2, 0, 3))

            def shade_rows(feature_rows):
                return render_row(feature_rows, in_use, depth_order, row_index, goal_image)
            total_loss, pull_row, rendered = jax.vjp(shade_rows, gathered, has_aux=True)
            grad_rows, = pull_row(jnp.ones((), jnp.float32))
            grad_rows = grad_rows * in_use[:, :, None, None]
            grad_rows = jnp.transpose(grad_rows, (2, 0, 1, 3)).reshape(9, TILES_DEV * KMAX, BLK)
            return (totals.at[:, safe_ids].add(grad_rows), rendered)
        initial = jnp.zeros((9, block_count, BLK), jnp.float32)
        summed, row_images = lax.scan(one_row, initial, jnp.arange(N_GS, dtype=jnp.int32))
        images.append(row_images.reshape(TILES, 3, TILE_PIX))
        grad_view, = pullback(summed.reshape(9, columns))
        gradient = gradient + grad_view
    new_params, new_first, new_second = apply_adam(gauss_params, first_moment, second_moment, gradient)
    return (new_params, new_first, new_second, jnp.stack(images))
```

```python
import functools
import math

import jax
import jax.numpy as jnp
from jax import lax
from jax.experimental import pallas as pl
from jax.experimental.pallas import tpu as pltpu
from jax.sharding import PartitionSpec as P

PARAMS = 59
BLK = 128
PIX = 256
FEATS = 9
CAP = 2
ADAM_STEP = 20

beta_one = 0.9
beta_two = 0.999
learn_rate = 0.01
adam_eps = 1e-08
dilation = 0.3
LOG2E = 1.4426950408889634
TINY = 1.1754944e-38
BELOW_ONE = 0.99999994

VMEM = pl.BlockSpec(memory_space=pltpu.VMEM)
SMEM = pl.BlockSpec(memory_space=pltpu.SMEM)


def params_of(megabytes):
    return pltpu.CompilerParams(vmem_limit_bytes=megabytes << 20)


def harmonics(x, y, z):
    square_x, square_y, square_z = (x * x, y * y, z * z)
    return [
        0.28209479177387814 + 0.0 * x,
        -0.4886025119029199 * y,
        0.4886025119029199 * z,
        -0.4886025119029199 * x,
        1.0925484305920792 * x * y,
        -1.0925484305920792 * y * z,
        0.31539156525252005 * (2.0 * square_z - square_x - square_y),
        -1.0925484305920792 * x * z,
        0.5462742152960396 * (square_x - square_y),
        -0.5900435899266435 * y * (3.0 * square_x - square_y),
        2.890611442640554 * x * y * z,
        -0.4570457994644658 * y * (4.0 * square_z - square_x - square_y),
        0.3731763325901154 * z * (2.0 * square_z - 3.0 * square_x - 3.0 * square_y),
        -0.4570457994644658 * x * (4.0 * square_z - square_x - square_y),
        1.445305721320277 * z * (square_x - square_y),
        -0.5900435899266435 * x * (square_x - 3.0 * square_y),
    ]


def geometry(rows, camera):
    sin_yaw, cos_yaw, sin_tilt, cos_tilt, shift_x, shift_y = camera
    right_axis = (cos_yaw, 0.0 * cos_yaw, -sin_yaw)
    upward = (sin_yaw * sin_tilt, cos_tilt, cos_yaw * sin_tilt)
    across = (
        16.0 * (right_axis[0] * rows[0] + right_axis[1] * rows[1] + right_axis[2] * rows[2])
        + shift_x
    )
    downward = 16.0 * (upward[0] * rows[0] + upward[1] * rows[1] + upward[2] * rows[2]) + shift_y
    scales = [jnp.exp(rows[3]), jnp.exp(rows[4]), jnp.exp(rows[5])]
    w, x, y, z = rows[6:10]
    inverse = lax.rsqrt(jnp.maximum(w * w + x * x + y * y + z * z, 1.0))
    w, x, y, z = (w * inverse, x * inverse, y * inverse, z * inverse)
    rotation = (
        (1.0 - 2.0 * (y * y + z * z), 2.0 * (x * y - w * z), 2.0 * (x * z + w * y)),
        (2.0 * (x * y + w * z), 1.0 - 2.0 * (x * x + z * z), 2.0 * (y * z - w * x)),
        (2.0 * (x * z - w * y), 2.0 * (y * z + w * x), 1.0 - 2.0 * (x * x + y * y)),
    )
    first, second = [
        [
            16.0
            * scales[k]
            * (
                direction[0] * rotation[0][k]
                + direction[1] * rotation[1][k]
                + direction[2] * rotation[2][k]
            )
            for k in range(3)
        ]
        for direction in (right_axis, upward)
    ]
    spread_first = first[0] * first[0] + first[1] * first[1] + first[2] * first[2] + dilation
    spread_mixed = first[0] * second[0] + first[1] * second[1] + first[2] * second[2]
    spread_second = second[0] * second[0] + second[1] * second[1] + second[2] * second[2] + dilation
    determinant = spread_first * spread_second - spread_mixed * spread_mixed
    return [
        across,
        downward,
        spread_second / determinant,
        -spread_mixed / determinant,
        spread_first / determinant,
    ]


def split(value, parts):
    out = []
    for _ in range(parts - 1):
        high = value.astype(jnp.bfloat16).astype(jnp.float32)
        out.append(high)
        value = value - high
    out.append(value)
    return out


def request_kernel(blocks_ref, order_ref, wanted_ref, table_ref, count_ref, held_ref):
    holders = wanted_ref.shape[0]
    tiles, slots = blocks_ref.shape
    per_holder = 64

    def clear(h, _):
        wanted_ref[h, 0, 0] = -1
        wanted_ref[h, 0, 1] = -1
        held_ref[h] = 0
        return 0

    lax.fori_loop(0, holders, clear, 0)

    def tile(t, _):
        def slot(i, used):
            block = blocks_ref[t, order_ref[t, i]]
            holder = lax.max(block, 0) // per_holder
            position = held_ref[holder]

            @pl.when(block >= 0)
            def _():
                held_ref[holder] = position + 1
                wanted_ref[holder, 0, position] = block - holder * per_holder
                table_ref[t, used] = holder * CAP + position

            return used + (block >= 0).astype(jnp.int32)

        count_ref[t] = lax.fori_loop(0, slots, slot, jnp.int32(0))
        return 0

    lax.fori_loop(0, tiles, tile, 0)


def project_kernel(camera_ref, params_ref, feats_ref, turned):
    blocks = feats_ref.shape[0]
    sin_yaw, cos_yaw, sin_tilt, cos_tilt = [camera_ref[k] for k in range(4)]
    camera = [camera_ref[k] for k in range(6)]
    terms = harmonics(sin_yaw * cos_tilt, -sin_tilt, cos_yaw * cos_tilt)
    row = lax.broadcasted_iota(jnp.int32, (8, PARAMS), 0)
    column = lax.broadcasted_iota(jnp.int32, (8, PARAMS), 1)
    which = column - 11 - 16 * row
    weight = jnp.zeros((8, PARAMS), jnp.float32)
    for j in range(16):
        weight = jnp.where((which == j) & (row < 3), terms[j], weight)
    for j in range(blocks):
        turned[j] = params_ref[0:16, j * BLK : (j + 1) * BLK]
    chunk = 8 * BLK
    for g in range(blocks // 8):
        shade = 0.5 + jnp.dot(
            weight,
            params_ref[:, g * chunk : (g + 1) * chunk],
            precision=lax.Precision.HIGHEST,
            preferred_element_type=jnp.float32,
        )
        mask = jnp.where(shade > 0.0, 1.0, jnp.where(shade == 0.0, 0.5, 0.0))
        shade = jnp.maximum(shade, 0.0)
        for j in range(8):
            feats_ref[8 * g + j, 6:9, :] = shade[0:3, j * BLK : (j + 1) * BLK]
            feats_ref[8 * g + j, 9:12, :] = mask[0:3, j * BLK : (j + 1) * BLK]
        rows = [turned[8 * g : 8 * g + 8, r, :] for r in range(11)]
        shaped = geometry(rows, camera)
        opacity = 1.0 / (1.0 + jnp.exp(-rows[10]))
        for r, value in enumerate(shaped + [opacity]):
            feats_ref[8 * g : 8 * g + 8, r, :] = value


def pick_kernel(asked_ref, feats_ref, out_ref):
    def one(h, _):
        for c in range(CAP):
            block = lax.max(asked_ref[h, 0, c], 0)
            out_ref[h, :, c, :] = feats_ref[block][0:FEATS]
        return 0

    lax.fori_loop(0, out_ref.shape[0], one, 0)


def bands(lower):
    row = lax.broadcasted_iota(jnp.int32, (BLK, 2 * BLK), 0)
    column = lax.broadcasted_iota(jnp.int32, (BLK, 2 * BLK), 1) % BLK
    inside = column < row if lower else column > row
    return inside.astype(jnp.float32).astype(jnp.bfloat16)


def nt(a, b):
    return lax.dot_general(a, b, (((1,), (1,)), ((), ())), preferred_element_type=jnp.float32)


def render_kernel(
    table_ref,
    count_ref,
    arrived_ref,
    goal_ref,
    image_ref,
    back_ref,
    before,
    after,
    basis,
    alphas,
    weights,
    halves,
    coefs,
):
    my_row = lax.axis_index("gs")
    before[...] = bands(True)
    after[...] = bands(False)
    pixel = lax.broadcasted_iota(jnp.int32, (8, PIX), 1)
    place = lax.broadcasted_iota(jnp.int32, (8, PIX), 0)
    x = (pixel % 16).astype(jnp.float32) - 7.5
    y = (pixel // 16).astype(jnp.float32) - 7.5
    terms = jnp.where(place == 0, 1.0, 0.0)
    for k, value in enumerate((x, y, x * x, x * y, y * y)):
        terms = jnp.where(place == k + 1, value, terms)
    basis[0:8] = terms
    basis[8:16] = terms
    basis[16:24] = terms
    basis[24:48] = jnp.zeros((24, PIX), jnp.float32)
    back_ref[...] = jnp.zeros_like(back_ref)
    zero = jnp.zeros((1, BLK), jnp.float32)

    def fetch(t, i):
        slot = table_ref[t, i]
        holder, place = slot // CAP, slot % CAP
        rows = [arrived_ref[holder, f, pl.ds(place, 1), :] for f in range(FEATS)]
        rows[0] = rows[0] - (16 * t + 8).astype(jnp.float32)
        rows[1] = rows[1] - (16 * my_row + 8).astype(jnp.float32)
        return holder, place, rows

    def tile(t, _):
        used = count_ref[t]

        def forward(i, carry):
            logs, image = carry
            _, _, (u, v, a, b, c, opacity, red, green, blue) = fetch(t, i)
            au, bv = (a * u + b * v, b * u + c * v)
            ks = [
                jnp.log2(jnp.maximum(opacity, TINY)) - (0.5 * LOG2E) * (au * u + bv * v),
                LOG2E * au,
                LOG2E * bv,
                (-0.5 * LOG2E) * a,
                -LOG2E * b,
                (-0.5 * LOG2E) * c,
                zero,
                zero,
            ]
            geo = split(jnp.concatenate(ks, axis=0), 3)
            high, mid, low = split(jnp.concatenate([red, green, blue] + [zero] * 5, axis=0), 3)
            stack = jnp.concatenate(
                geo + [
                    high[0:3], high[0:3], mid[0:3], high[0:3], low[0:3], mid[0:3],
                    jnp.zeros((6, BLK), jnp.float32),
                ],
                axis=0,
            )
            turned = stack.T.astype(jnp.bfloat16)
            coefs[i] = turned
            alpha = jnp.exp2(
                jnp.dot(turned, basis[...].astype(jnp.bfloat16), preferred_element_type=jnp.float32)
            )
            alpha = jnp.minimum(alpha, BELOW_ONE)
            alphas[i] = alpha
            loss = jnp.log2(1.0 - alpha)
            pair = jnp.concatenate([q.astype(jnp.bfloat16) for q in split(loss, 2)], axis=0)
            run = jnp.dot(before[...], pair, preferred_element_type=jnp.float32)
            weight = alpha * jnp.exp2(run + logs)
            weights[i] = weight
            pair = jnp.concatenate([q.astype(jnp.bfloat16) for q in split(weight, 2)], axis=0)
            halves[i] = pair
            colours = stack[24:48].astype(jnp.bfloat16)
            shade = jnp.dot(
                jnp.concatenate([colours, colours], axis=1), pair, preferred_element_type=jnp.float32
            )
            image = image + (shade[0:3] + (shade[6:9] + shade[12:15]))
            logs = logs + (run[BLK - 1 : BLK] + loss[BLK - 1 : BLK])
            return logs, image

        _, image = lax.fori_loop(
            0, used, forward,
            (jnp.zeros((1, PIX), jnp.float32), jnp.zeros((3, PIX), jnp.float32)),
        )
        image_ref[t] = image
        pull = image - goal_ref[t]
        high, mid, low = split(pull, 3)
        pulls = jnp.concatenate(
            [high, mid, high, low, high, mid, jnp.zeros((6, PIX), jnp.float32)], axis=0
        )
        basis[24:48] = pulls
        pulled = jnp.concatenate([jnp.zeros((24, PIX), jnp.float32), pulls], axis=0).astype(
            jnp.bfloat16
        )
        colour_pulls = jnp.concatenate(
            [high, mid, low, jnp.zeros((7, PIX), jnp.float32)], axis=0
        ).astype(jnp.bfloat16)
        moments_of = basis[0:16].astype(jnp.bfloat16)

        def backward(step, later):
            i = used - 1 - step
            holder, place, (u, v, a, b, c, _, _, _, _) = fetch(t, i)
            reach = jnp.dot(coefs[i], pulled, preferred_element_type=jnp.float32) * weights[i]
            pair = jnp.concatenate([q.astype(jnp.bfloat16) for q in split(reach, 2)], axis=0)
            behind = jnp.dot(after[...], pair, preferred_element_type=jnp.float32)
            alpha = alphas[i]
            push = reach - (behind + later) * (alpha / (1.0 - alpha))
            trio = jnp.concatenate([q.astype(jnp.bfloat16) for q in split(push, 3)], axis=0)
            moments = nt(moments_of, trio)
            moments = moments[:, 0:BLK] + (moments[:, BLK : 2 * BLK] + moments[:, 2 * BLK :])
            tints = nt(colour_pulls, halves[i])
            tints = tints[:, 0:BLK] + tints[:, BLK:]
            tints = tints[0:3] + (tints[3:6] + tints[6:9])
            m0, mx, my, mxx, mxy, myy = [moments[k : k + 1] for k in range(6)]
            cx, cy = (mx - u * m0, my - v * m0)
            grads = [
                a * cx + b * cy,
                b * cx + c * cy,
                -0.5 * (mxx - u * (mx + cx)),
                -(mxy - u * my - v * cx),
                -0.5 * (myy - v * (my + cy)),
                m0,
                tints[0:1],
                tints[1:2],
                tints[2:3],
            ]
            for f, value in enumerate(grads):
                back_ref[holder, f, pl.ds(place, 1), :] = value
            return later + (behind[0:1] + reach[0:1])

        lax.fori_loop(0, used, backward, jnp.zeros((1, PIX), jnp.float32))
        basis[24:48] = jnp.zeros((24, PIX), jnp.float32)
        return 0

    lax.fori_loop(0, image_ref.shape[0], tile, 0)


def land_kernel(asked_ref, camera_ref, landed_ref, feats_ref, out_ref, total):
    total[...] = jnp.zeros_like(total)

    def one(h, _):
        for c in range(CAP):
            block = asked_ref[h, 0, c]

            @pl.when(block >= 0)
            def _():
                total[block, 0:FEATS, :] = total[block, 0:FEATS, :] + landed_ref[h, :, c, :]

        return 0

    lax.fori_loop(0, landed_ref.shape[0], one, 0)
    groups = total.shape[0] // 8
    for g in range(groups):
        for f in range(FEATS):
            value = total[8 * g : 8 * g + 8, f, :]
            if f >= 6:
                value = value * feats_ref[8 * g : 8 * g + 8, f + 3, :]
            out_ref[g, f] = value
    place = lax.broadcasted_iota(jnp.int32, (8, BLK), 0)
    shown = jnp.zeros((8, BLK), jnp.float32)
    for k in range(6):
        shown = jnp.where(place == k, camera_ref[k], shown)
    for g in range(groups):
        out_ref[g, FEATS] = shown


def adam(weights_in, moment_one, moment_two, gradient):
    new_first = beta_one * moment_one + (1.0 - beta_one) * gradient
    new_second = beta_two * moment_two + (1.0 - beta_two) * gradient * gradient
    step_size = learn_rate / (1.0 - beta_one**ADAM_STEP)
    new_params = weights_in - step_size * new_first / (
        jnp.sqrt(new_second / (1.0 - beta_two**ADAM_STEP)) + adam_eps
    )
    return (new_params, new_first, new_second)


def update_kernel(
    params_ref, first_ref, second_ref, own_ref, next_ref, across_ref, last_ref,
    new_params_ref, new_first_ref, new_second_ref, pulls, turned, shades, waves,
):
    me = lax.axis_index("view")
    views = 4
    for k, ref in enumerate((own_ref, next_ref, across_ref, last_ref)):
        pulls[(me + k) % views] = ref[0]
    for j in range(8):
        turned[j] = params_ref[0:16, j * BLK : (j + 1) * BLK]
    rows = [turned[:, r, :] for r in range(11)]
    opacity = 1.0 / (1.0 + jnp.exp(-rows[10]))
    total = [None] * 11
    for v in range(views):
        camera = [pulls[v, FEATS, k : k + 1, :] for k in range(6)]
        _, pull_back = jax.vjp(lambda *r: geometry(r, camera), *rows[0:10])
        grads = list(pull_back([pulls[v, f] for f in range(5)]))
        grads.append(pulls[v, 5] * (1.0 - opacity))
        total = grads if v == 0 else [p + q for p, q in zip(total, grads)]
        for c in range(3):
            shades[:, 3 * v + c, :] = pulls[v, 6 + c]

        @pl.when(pl.program_id(0) == 0)
        def _():
            sin_yaw, cos_yaw, sin_tilt, cos_tilt = camera[0:4]
            terms = harmonics(sin_yaw * cos_tilt, -sin_tilt, cos_yaw * cos_tilt)
            for k in range(8):
                row = lax.broadcasted_iota(jnp.int32, (8, BLK), 0) + (8 * k - 11)
                wave = jnp.zeros((8, BLK), jnp.float32)
                for j in range(16):
                    wave = jnp.where((row >= 0) & (row % 16 == j), terms[j], wave)
                waves[v, 8 * k : 8 * k + 8, :] = wave

    for r in range(11):
        turned[:, r, :] = total[r]
    row_in = lax.broadcasted_iota(jnp.int32, (8, BLK), 0)
    for j in range(8):
        columns = slice(j * BLK, (j + 1) * BLK)
        for k in range(8):
            gradient = None
            if k > 0:
                first = (8 * k - 11) // 16 if k > 1 else 0
                last = min((8 * k + 7 - 11) // 16, 2)
                for v in range(views):
                    tint = shades[j, 3 * v + first : 3 * v + first + 1, :]
                    if last != first:
                        tint = jnp.where(
                            row_in + (8 * k - 11) < 16 * last,
                            tint,
                            shades[j, 3 * v + last : 3 * v + last + 1, :],
                        )
                    term = waves[v, 8 * k : 8 * k + 8, :] * tint
                    gradient = term if gradient is None else gradient + term
            if k == 0:
                gradient = turned[j, 0:8, :]
            if k == 1:
                gradient = jnp.where(row_in < 3, turned[j, 8:16, :], gradient)
            height = min(8, PARAMS - 8 * k)
            at = (slice(8 * k, 8 * k + height), columns)
            values = adam(params_ref[at], first_ref[at], second_ref[at], gradient[0:height])
            new_params_ref[at], new_first_ref[at], new_second_ref[at] = values


def shards(
    gauss_params, first_moment, second_moment, view_pose, tile_blocks, tile_order, target_image
):
    groups = lax.axis_size("gs")
    views = lax.axis_size("view")
    columns = gauss_params.shape[1]
    blocks = columns // BLK
    tiles, slots = tile_blocks.shape[1:]
    f32, i32 = jnp.float32, jnp.int32
    shape = jax.ShapeDtypeStruct
    pose = view_pose[0]
    camera = jnp.concatenate(
        [jnp.stack([jnp.sin(pose[0]), jnp.cos(pose[0]), jnp.sin(pose[1]), jnp.cos(pose[1])]), pose[2:4]]
    )

    wanted, table, count = pl.pallas_call(
        request_kernel,
        out_shape=[shape((groups, 1, CAP), i32), shape((tiles, slots), i32), shape((tiles,), i32)],
        in_specs=[SMEM, SMEM],
        out_specs=[SMEM, SMEM, SMEM],
        scratch_shapes=[pltpu.SMEM((groups,), i32)],
        name="requests",
    )(tile_blocks[0], tile_order[0])
    asked = lax.all_to_all(wanted, "gs", split_axis=0, concat_axis=0, tiled=True)
    feats = pl.pallas_call(
        project_kernel,
        out_shape=shape((blocks, 16, BLK), f32),
        in_specs=[SMEM, VMEM],
        out_specs=VMEM,
        scratch_shapes=[pltpu.VMEM((blocks, 16, BLK), f32)],
        compiler_params=params_of(24),
        name="project",
    )(camera, gauss_params)
    outgoing = pl.pallas_call(
        pick_kernel,
        out_shape=shape((groups, FEATS, CAP, BLK), f32),
        in_specs=[SMEM, VMEM],
        out_specs=VMEM,
        compiler_params=params_of(16),
        name="pick",
    )(asked, feats)
    arrived = lax.all_to_all(outgoing, "gs", split_axis=0, concat_axis=0, tiled=True)
    image, back = pl.pallas_call(
        render_kernel,
        out_shape=[shape((tiles, 3, PIX), f32), shape((groups, FEATS, CAP, BLK), f32)],
        in_specs=[SMEM, SMEM, VMEM, VMEM],
        out_specs=[VMEM, VMEM],
        scratch_shapes=[
            pltpu.VMEM((BLK, 2 * BLK), jnp.bfloat16),
            pltpu.VMEM((BLK, 2 * BLK), jnp.bfloat16),
            pltpu.VMEM((48, PIX), f32),
            pltpu.VMEM((slots, BLK, PIX), f32),
            pltpu.VMEM((slots, BLK, PIX), f32),
            pltpu.VMEM((slots, 2 * BLK, PIX), jnp.bfloat16),
            pltpu.VMEM((slots, BLK, 48), jnp.bfloat16),
        ],
        compiler_params=params_of(32),
        name="render",
    )(table, count, arrived, target_image[0])
    landed = lax.all_to_all(back, "gs", split_axis=0, concat_axis=0, tiled=True)
    own = pl.pallas_call(
        land_kernel,
        out_shape=shape((blocks // 8, FEATS + 1, 8, BLK), f32),
        in_specs=[SMEM, SMEM, VMEM, VMEM],
        out_specs=VMEM,
        scratch_shapes=[pltpu.VMEM((blocks, 16, BLK), f32)],
        compiler_params=params_of(16),
        name="land",
    )(asked, camera, landed, feats)
    others = [
        lax.ppermute(own, "view", [((i + k) % views, i) for i in range(views)]) for k in range(1, views)
    ]
    chunk = 8 * BLK
    wide = pl.BlockSpec((PARAMS, chunk), lambda i: (0, i))
    deep = pl.BlockSpec((1, FEATS + 1, 8, BLK), lambda i: (i, 0, 0, 0))
    new_params, new_first, new_second = pl.pallas_call(
        update_kernel,
        grid=(columns // chunk,),
        out_shape=[shape((PARAMS, columns), f32)] * 3,
        in_specs=[wide] * 3 + [deep] * 4,
        out_specs=[wide] * 3,
        scratch_shapes=[
            pltpu.VMEM((views, FEATS + 1, 8, BLK), f32),
            pltpu.VMEM((8, 16, BLK), f32),
            pltpu.VMEM((8, 16, BLK), f32),
            pltpu.VMEM((views, 64, BLK), f32),
        ],
        compiler_params=params_of(24),
        name="update",
    )(gauss_params, first_moment, second_moment, own, *others)
    return (new_params, new_first, new_second, image[None])


def solution(mesh):
    placed = (
        P(None, "gs"),
        P(None, "gs"),
        P(None, "gs"),
        P("view", None),
        P("view", "gs", None),
        P("view", "gs", None),
        P("view", "gs", None, None),
    )
    return jax.shard_map(
        shards,
        mesh=mesh,
        in_specs=placed,
        out_specs=(P(None, "gs"), P(None, "gs"), P(None, "gs"), P("view", "gs", None, None)),
        check_vma=False,
    )
```

```python
import functools
import math

import jax
import jax.numpy as jnp
from jax import lax
from jax.experimental import pallas as pl
from jax.experimental.pallas import tpu as pltpu
from jax.sharding import PartitionSpec as P

PARAMS = 59
BLK = 128
PIX = 256
FEATS = 9
CAP = 2
ADAM_STEP = 20

beta_one = 0.9
beta_two = 0.999
learn_rate = 0.01
adam_eps = 1e-08
dilation = 0.3
LOG2E = 1.4426950408889634
TINY = 1.1754944e-38
BELOW_ONE = 0.99999994

VMEM = pl.BlockSpec(memory_space=pltpu.VMEM)
SMEM = pl.BlockSpec(memory_space=pltpu.SMEM)


def params_of(megabytes):
    return pltpu.CompilerParams(vmem_limit_bytes=megabytes << 20)


def harmonics(x, y, z):
    square_x, square_y, square_z = (x * x, y * y, z * z)
    return [
        0.28209479177387814 + 0.0 * x,
        -0.4886025119029199 * y,
        0.4886025119029199 * z,
        -0.4886025119029199 * x,
        1.0925484305920792 * x * y,
        -1.0925484305920792 * y * z,
        0.31539156525252005 * (2.0 * square_z - square_x - square_y),
        -1.0925484305920792 * x * z,
        0.5462742152960396 * (square_x - square_y),
        -0.5900435899266435 * y * (3.0 * square_x - square_y),
        2.890611442640554 * x * y * z,
        -0.4570457994644658 * y * (4.0 * square_z - square_x - square_y),
        0.3731763325901154 * z * (2.0 * square_z - 3.0 * square_x - 3.0 * square_y),
        -0.4570457994644658 * x * (4.0 * square_z - square_x - square_y),
        1.445305721320277 * z * (square_x - square_y),
        -0.5900435899266435 * x * (square_x - 3.0 * square_y),
    ]


def geometry(rows, camera):
    sin_yaw, cos_yaw, sin_tilt, cos_tilt, shift_x, shift_y = camera
    right_axis = (cos_yaw, 0.0 * cos_yaw, -sin_yaw)
    upward = (sin_yaw * sin_tilt, cos_tilt, cos_yaw * sin_tilt)
    across = (
        16.0 * (right_axis[0] * rows[0] + right_axis[1] * rows[1] + right_axis[2] * rows[2])
        + shift_x
    )
    downward = 16.0 * (upward[0] * rows[0] + upward[1] * rows[1] + upward[2] * rows[2]) + shift_y
    scales = [jnp.exp(rows[3]), jnp.exp(rows[4]), jnp.exp(rows[5])]
    w, x, y, z = rows[6:10]
    inverse = lax.rsqrt(jnp.maximum(w * w + x * x + y * y + z * z, 1.0))
    w, x, y, z = (w * inverse, x * inverse, y * inverse, z * inverse)
    rotation = (
        (1.0 - 2.0 * (y * y + z * z), 2.0 * (x * y - w * z), 2.0 * (x * z + w * y)),
        (2.0 * (x * y + w * z), 1.0 - 2.0 * (x * x + z * z), 2.0 * (y * z - w * x)),
        (2.0 * (x * z - w * y), 2.0 * (y * z + w * x), 1.0 - 2.0 * (x * x + y * y)),
    )
    first, second = [
        [
            16.0
            * scales[k]
            * (
                direction[0] * rotation[0][k]
                + direction[1] * rotation[1][k]
                + direction[2] * rotation[2][k]
            )
            for k in range(3)
        ]
        for direction in (right_axis, upward)
    ]
    spread_first = first[0] * first[0] + first[1] * first[1] + first[2] * first[2] + dilation
    spread_mixed = first[0] * second[0] + first[1] * second[1] + first[2] * second[2]
    spread_second = second[0] * second[0] + second[1] * second[1] + second[2] * second[2] + dilation
    determinant = spread_first * spread_second - spread_mixed * spread_mixed
    return [
        across,
        downward,
        spread_second / determinant,
        -spread_mixed / determinant,
        spread_first / determinant,
    ]


def split(value, parts):
    out = []
    for _ in range(parts - 1):
        high = value.astype(jnp.bfloat16).astype(jnp.float32)
        out.append(high)
        value = value - high
    out.append(value)
    return out


def request_kernel(blocks_ref, order_ref, wanted_ref, table_ref, count_ref, held_ref):
    holders = wanted_ref.shape[0]
    tiles, slots = blocks_ref.shape
    per_holder = 64

    def clear(h, _):
        wanted_ref[h, 0, 0] = -1
        wanted_ref[h, 0, 1] = -1
        held_ref[h] = 0
        return 0

    lax.fori_loop(0, holders, clear, 0)

    def tile(t, _):
        def slot(i, used):
            block = blocks_ref[t, order_ref[t, i]]
            holder = lax.max(block, 0) // per_holder
            position = held_ref[holder]

            @pl.when(block >= 0)
            def _():
                held_ref[holder] = position + 1
                wanted_ref[holder, 0, position] = block - holder * per_holder
                table_ref[t, used] = holder * CAP + position

            return used + (block >= 0).astype(jnp.int32)

        count_ref[t] = lax.fori_loop(0, slots, slot, jnp.int32(0))
        return 0

    lax.fori_loop(0, tiles, tile, 0)


def project_kernel(camera_ref, params_ref, feats_ref, turned):
    blocks = feats_ref.shape[0]
    sin_yaw, cos_yaw, sin_tilt, cos_tilt = [camera_ref[k] for k in range(4)]
    camera = [camera_ref[k] for k in range(6)]
    terms = harmonics(sin_yaw * cos_tilt, -sin_tilt, cos_yaw * cos_tilt)
    row = lax.broadcasted_iota(jnp.int32, (8, PARAMS), 0)
    column = lax.broadcasted_iota(jnp.int32, (8, PARAMS), 1)
    which = column - 11 - 16 * row
    weight = jnp.zeros((8, PARAMS), jnp.float32)
    for j in range(16):
        weight = jnp.where((which == j) & (row < 3), terms[j], weight)
    for j in range(blocks):
        turned[j] = params_ref[0:16, j * BLK : (j + 1) * BLK]
    chunk = 8 * BLK
    for g in range(blocks // 8):
        shade = 0.5 + jnp.dot(
            weight,
            params_ref[:, g * chunk : (g + 1) * chunk],
            precision=lax.Precision.HIGHEST,
            preferred_element_type=jnp.float32,
        )
        mask = jnp.where(shade > 0.0, 1.0, jnp.where(shade == 0.0, 0.5, 0.0))
        shade = jnp.maximum(shade, 0.0)
        for j in range(8):
            feats_ref[8 * g + j, 6:9, :] = shade[0:3, j * BLK : (j + 1) * BLK]
            feats_ref[8 * g + j, 9:12, :] = mask[0:3, j * BLK : (j + 1) * BLK]
        rows = [turned[8 * g : 8 * g + 8, r, :] for r in range(11)]
        shaped = geometry(rows, camera)
        opacity = 1.0 / (1.0 + jnp.exp(-rows[10]))
        for r, value in enumerate(shaped + [opacity]):
            feats_ref[8 * g : 8 * g + 8, r, :] = value


def pick_kernel(asked_ref, feats_ref, out_ref):
    def one(h, _):
        for c in range(CAP):
            block = lax.max(asked_ref[h, 0, c], 0)
            out_ref[h, :, c, :] = feats_ref[block][0:FEATS]
        return 0

    lax.fori_loop(0, out_ref.shape[0], one, 0)


def bands(earlier):
    row = lax.broadcasted_iota(jnp.int32, (4 * BLK, 2 * BLK), 0) % (2 * BLK)
    column = lax.broadcasted_iota(jnp.int32, (4 * BLK, 2 * BLK), 1)
    inside = row < column if earlier else row > column
    return inside.astype(jnp.float32).astype(jnp.bfloat16)


def halves_of(value):
    high = value.astype(jnp.bfloat16)
    low = (value - high.astype(jnp.float32)).astype(jnp.bfloat16)
    return jnp.concatenate([high, low], axis=1)


def sums_by(values, band):
    rows = values[0].shape[0]
    halves = jnp.concatenate([halves_of(value) for value in values], axis=0)
    total = jnp.dot(halves, band[...], preferred_element_type=jnp.float32)
    return [total[rows * h : rows * (h + 1)] for h in range(len(values))]


def twice(value):
    return jnp.concatenate([value, value], axis=1)


def fold(value):
    return jnp.sum(value.reshape(-1, 8, BLK), axis=0)


def render_kernel(
    table_ref,
    count_ref,
    arrived_ref,
    goal_ref,
    image_ref,
    back_ref,
    ranked,
    before,
    after,
    basis,
    *buffers,
):
    my_row = lax.axis_index("gs")
    lanes = tuple(buffers[h::4] for h in range(4))
    tiles, slots = table_ref.shape
    before[...] = bands(True)
    after[...] = bands(False)
    pixel = lax.broadcasted_iota(jnp.int32, (PIX, 48), 0)
    place = lax.broadcasted_iota(jnp.int32, (PIX, 48), 1)
    x = (pixel % 16).astype(jnp.float32) - 7.5
    y = (pixel // 16).astype(jnp.float32) - 7.5
    powers = jnp.where((place < 24) & (place % 8 == 0), 1.0, 0.0)
    for k, value in enumerate((x, y, x * x, x * y, y * y)):
        powers = jnp.where((place < 24) & (place % 8 == k + 1), value, powers)
    basis[...] = powers.astype(jnp.bfloat16)
    x = lax.broadcasted_iota(jnp.int32, (16, BLK), 0).astype(jnp.float32) - 7.5
    blank = jnp.zeros((8, PIX), jnp.float32)
    back_ref[...] = jnp.zeros_like(back_ref)
    slot_at = lax.broadcasted_iota(jnp.int32, (slots, BLK), 0)
    for _, terms, *_ in lanes:
        terms[...] = jnp.zeros_like(terms)
    counts = [count_ref[t] for t in range(tiles)]
    for t in range(tiles):
        rank = jnp.int32(0)
        for s in range(tiles):
            ahead = counts[s] >= counts[t] if s < t else counts[s] > counts[t]
            if s != t:
                rank = rank + ahead.astype(jnp.int32)
        ranked[rank] = t

    def side_by_side(ref, at, j):
        return jnp.concatenate(
            [ref[at, pl.ds(2 * j + k, 1), :].reshape(-1, BLK) for k in range(2)], axis=1
        )

    def local(t, rows):
        u = rows[0] - (16 * t + 8).astype(jnp.float32)
        v = rows[1] - (16 * my_row + 8).astype(jnp.float32)
        return u, v, rows[2], rows[3], rows[4]

    def prepare(t, used, rows, terms):
        for i in range(slots):
            slot = jnp.where(i < used, table_ref[t, i], 0)
            holder, place = slot // CAP, slot % CAP
            for f in range(FEATS):
                rows[f, i : i + 1, :] = arrived_ref[holder, f, pl.ds(place, 1), :]
        u, v, a, b, d = local(t, rows)
        au, bv = (a * u + b * v, b * u + d * v)
        full = jnp.log2(jnp.maximum(rows[5], TINY)) - (0.5 * LOG2E) * (au * u + bv * v)
        shape = [full, LOG2E * au, LOG2E * bv, (-0.5 * LOG2E) * a, -LOG2E * b, (-0.5 * LOG2E) * d]
        for k, value in enumerate(shape):
            value = jnp.where(slot_at < used, value, -2e4 if k == 0 else 0.0)
            for p, part in enumerate(split(value, 3)):
                terms[8 * p + k] = part
        for k in range(3):
            tint = jnp.where(slot_at < used, rows[6 + k], 0.0)
            rows[6 + k] = tint
            high, mid, low = split(tint, 3)
            for p, part in enumerate((high, high, mid, high, low, mid)):
                terms[24 + 3 * p + k] = part

    def tile_pair(g, _):
        chosen = [ranked[4 * g + h] for h in range(4)]
        used = [count_ref[t] for t in chosen]
        pairs = (functools.reduce(lax.max, used) + 1) // 2
        for h, (rows, terms, _, _, shades, _, _) in enumerate(lanes):
            prepare(chosen[h], used[h], rows, terms)
            shades[...] = jnp.zeros_like(shades)

        def forward(j, logs):
            state = []
            for rows, terms, *_ in lanes:
                coefs = side_by_side(terms, slice(None), j).astype(jnp.bfloat16)
                state.append(jnp.dot(basis[...], coefs, preferred_element_type=jnp.float32))
            state = [jnp.minimum(jnp.exp2(value), BELOW_ONE) for value in state]
            losses = [jnp.log2(1.0 - alpha) for alpha in state]
            runs = sums_by(losses, before)
            out = []
            for h, (rows, _, ratios, weights, shades, _, _) in enumerate(lanes):
                alpha, loss, run = state[h], losses[h], runs[h]
                ratios[j] = alpha * jnp.exp2(-loss)
                weight = alpha * jnp.exp2(run + twice(logs[h]))
                weights[j] = weight
                tints = side_by_side(rows, slice(6, 9), j)
                for c in range(3):
                    shade = weight * tints[c : c + 1]
                    shades[c] += shade[:, 0:BLK] + shade[:, BLK:]
                last = run[:, 2 * BLK - 1 :] + loss[:, 2 * BLK - 1 :]
                out.append(logs[h] + jnp.broadcast_to(last, (PIX, BLK)))
            return tuple(out)

        still = jnp.zeros((PIX, BLK), jnp.float32)
        lax.fori_loop(0, pairs, forward, (still,) * 4)
        lane = lax.broadcasted_iota(jnp.int32, (PIX, BLK), 1)
        pulled = []
        for h, (_, _, _, _, shades, pulls, _) in enumerate(lanes):
            columns = jnp.zeros((PIX, BLK), jnp.float32)
            for c in range(3):
                columns = jnp.where(lane == c, jnp.sum(shades[c], axis=1, keepdims=True), columns)
            image = columns.T[0:3]
            image_ref[chosen[h]] = image
            pull = image - goal_ref[chosen[h]]
            high, mid, low = split(pull, 3)
            turned = jnp.concatenate(
                [blank] * 3 + [high, mid, high, low, high, mid, pull, blank[0:3]], axis=0
            ).T
            for c in range(3):
                pulls[c] = jnp.broadcast_to(turned[:, 42 + c : 43 + c], (PIX, BLK))
            pulled.append(turned.astype(jnp.bfloat16))

        def backward(step, later):
            j = pairs - 1 - step
            reaches = []
            for h, (_, terms, _, weights, *_) in enumerate(lanes):
                coefs = side_by_side(terms, slice(None), j).astype(jnp.bfloat16)
                reaches.append(
                    jnp.dot(pulled[h], coefs, preferred_element_type=jnp.float32) * weights[j]
                )
            behinds = sums_by(reaches, after)
            out = []
            for h, (_, _, ratios, weights, _, pulls, sums) in enumerate(lanes):
                reach, behind, weight = reaches[h], behinds[h], weights[j]
                push = reach - (behind + twice(later[h])) * ratios[j]
                for k in range(2):
                    at = slice(BLK * k, BLK * (k + 1))
                    slot = pl.ds(2 * j + k, 1)
                    part = push[:, at].reshape(16, 16, BLK)
                    plain, tilted, bent = (None, None, None)
                    for n in range(8):
                        y = 7.5 - n
                        even, odd = (part[15 - n] + part[n], y * (part[15 - n] - part[n]))
                        square = (y * y) * even
                        plain = even if n == 0 else plain + even
                        tilted = odd if n == 0 else tilted + odd
                        bent = square if n == 0 else bent + square
                    values = (plain, x * plain, tilted, x * x * plain, x * tilted, bent)
                    for f, value in enumerate(values):
                        sums[f, slot] = (value[0:8] + value[8:16]).reshape(1, 8, BLK)
                    for c in range(3):
                        sums[6 + c, slot] = fold(weight[:, at] * pulls[c]).reshape(1, 8, BLK)
                out.append(
                    later[h] + jnp.broadcast_to(behind[:, 0:1] + reach[:, 0:1], (PIX, BLK))
                )
            return tuple(out)

        lax.fori_loop(0, pairs, backward, (still,) * 4)
        for h, (rows, _, _, _, _, _, sums) in enumerate(lanes):
            t = chosen[h]
            u, v, a, b, d = local(t, rows)
            m0, mx, my, mxx, mxy, myy, red, green, blue = [
                sum(sums[f, :, s, :] for s in range(8)) for f in range(FEATS)
            ]
            cx, cy = (mx - u * m0, my - v * m0)
            rows[0] = a * cx + b * cy
            rows[1] = b * cx + d * cy
            rows[2] = -0.5 * (mxx - u * (mx + cx))
            rows[3] = -(mxy - u * my - v * cx)
            rows[4] = -0.5 * (myy - v * (my + cy))
            for f, value in ((5, m0), (6, red), (7, green), (8, blue)):
                rows[f] = value

            def send(i, _, t=t, rows=rows):
                slot = table_ref[t, i]
                holder, place = slot // CAP, slot % CAP
                for f in range(FEATS):
                    back_ref[holder, f, pl.ds(place, 1), :] = rows[f, pl.ds(i, 1), :]
                return 0

            lax.fori_loop(0, used[h], send, 0)
        return 0

    lax.fori_loop(0, tiles // 4, tile_pair, 0)


def render(table, count, arrived, goal):
    tiles, slots = table.shape
    groups = arrived.shape[0]
    f32 = jnp.float32
    shape = jax.ShapeDtypeStruct
    return pl.pallas_call(
        render_kernel,
        out_shape=[shape((tiles, 3, PIX), f32), shape((groups, FEATS, CAP, BLK), f32)],
        in_specs=[SMEM, SMEM, VMEM, VMEM],
        out_specs=[VMEM, VMEM],
        scratch_shapes=[
            pltpu.SMEM((tiles,), jnp.int32),
            pltpu.VMEM((4 * BLK, 2 * BLK), jnp.bfloat16),
            pltpu.VMEM((4 * BLK, 2 * BLK), jnp.bfloat16),
            pltpu.VMEM((PIX, 48), jnp.bfloat16),
        ]
        + [
            pltpu.VMEM(dims, f32)
            for dims in (
                (FEATS, slots, BLK),
                (48, slots, BLK),
                (slots // 2, PIX, 2 * BLK),
                (slots // 2, PIX, 2 * BLK),
                (3, PIX, BLK),
                (3, PIX, BLK),
                (FEATS, slots, 8, BLK),
            )
            for _ in range(4)
        ],
        compiler_params=params_of(48),
        name="render",
    )(table, count, arrived, goal)


def land_kernel(asked_ref, camera_ref, landed_ref, feats_ref, out_ref, total):
    total[...] = jnp.zeros_like(total)

    def one(h, _):
        for c in range(CAP):
            block = asked_ref[h, 0, c]

            @pl.when(block >= 0)
            def _():
                total[block, 0:FEATS, :] = total[block, 0:FEATS, :] + landed_ref[h, :, c, :]

        return 0

    lax.fori_loop(0, landed_ref.shape[0], one, 0)
    groups = total.shape[0] // 8
    for g in range(groups):
        for f in range(FEATS):
            value = total[8 * g : 8 * g + 8, f, :]
            if f >= 6:
                value = value * feats_ref[8 * g : 8 * g + 8, f + 3, :]
            out_ref[g, f] = value
    place = lax.broadcasted_iota(jnp.int32, (8, BLK), 0)
    shown = jnp.zeros((8, BLK), jnp.float32)
    for k in range(6):
        shown = jnp.where(place == k, camera_ref[k], shown)
    for g in range(groups):
        out_ref[g, FEATS] = shown


def adam(weights_in, moment_one, moment_two, gradient):
    new_first = beta_one * moment_one + (1.0 - beta_one) * gradient
    new_second = beta_two * moment_two + (1.0 - beta_two) * gradient * gradient
    step_size = learn_rate / (1.0 - beta_one**ADAM_STEP)
    new_params = weights_in - step_size * new_first / (
        jnp.sqrt(new_second / (1.0 - beta_two**ADAM_STEP)) + adam_eps
    )
    return (new_params, new_first, new_second)


def update_kernel(
    params_ref, first_ref, second_ref, own_ref, next_ref, across_ref, last_ref,
    new_params_ref, new_first_ref, new_second_ref, pulls, turned, shades, waves,
):
    me = lax.axis_index("view")
    views = 4
    for k, ref in enumerate((own_ref, next_ref, across_ref, last_ref)):
        pulls[(me + k) % views] = ref[0]
    for j in range(8):
        turned[j] = params_ref[0:16, j * BLK : (j + 1) * BLK]
    rows = [turned[:, r, :] for r in range(11)]
    opacity = 1.0 / (1.0 + jnp.exp(-rows[10]))
    total = [None] * 11
    for v in range(views):
        camera = [pulls[v, FEATS, k : k + 1, :] for k in range(6)]
        _, pull_back = jax.vjp(lambda *r: geometry(r, camera), *rows[0:10])
        grads = list(pull_back([pulls[v, f] for f in range(5)]))
        grads.append(pulls[v, 5] * (1.0 - opacity))
        total = grads if v == 0 else [p + q for p, q in zip(total, grads)]
        for c in range(3):
            shades[:, 3 * v + c, :] = pulls[v, 6 + c]

        @pl.when(pl.program_id(0) == 0)
        def _():
            sin_yaw, cos_yaw, sin_tilt, cos_tilt = camera[0:4]
            terms = harmonics(sin_yaw * cos_tilt, -sin_tilt, cos_yaw * cos_tilt)
            for k in range(8):
                row = lax.broadcasted_iota(jnp.int32, (8, BLK), 0) + (8 * k - 11)
                wave = jnp.zeros((8, BLK), jnp.float32)
                for j in range(16):
                    wave = jnp.where((row >= 0) & (row % 16 == j), terms[j], wave)
                waves[v, 8 * k : 8 * k + 8, :] = wave

    for r in range(11):
        turned[:, r, :] = total[r]
    row_in = lax.broadcasted_iota(jnp.int32, (8, BLK), 0)
    for j in range(8):
        columns = slice(j * BLK, (j + 1) * BLK)
        for k in range(8):
            gradient = None
            if k > 0:
                first = (8 * k - 11) // 16 if k > 1 else 0
                last = min((8 * k + 7 - 11) // 16, 2)
                for v in range(views):
                    tint = shades[j, 3 * v + first : 3 * v + first + 1, :]
                    if last != first:
                        tint = jnp.where(
                            row_in + (8 * k - 11) < 16 * last,
                            tint,
                            shades[j, 3 * v + last : 3 * v + last + 1, :],
                        )
                    term = waves[v, 8 * k : 8 * k + 8, :] * tint
                    gradient = term if gradient is None else gradient + term
            if k == 0:
                gradient = turned[j, 0:8, :]
            if k == 1:
                gradient = jnp.where(row_in < 3, turned[j, 8:16, :], gradient)
            height = min(8, PARAMS - 8 * k)
            at = (slice(8 * k, 8 * k + height), columns)
            values = adam(params_ref[at], first_ref[at], second_ref[at], gradient[0:height])
            new_params_ref[at], new_first_ref[at], new_second_ref[at] = values


def shards(
    gauss_params, first_moment, second_moment, view_pose, tile_blocks, tile_order, target_image
):
    groups = lax.axis_size("gs")
    views = lax.axis_size("view")
    columns = gauss_params.shape[1]
    blocks = columns // BLK
    tiles, slots = tile_blocks.shape[1:]
    f32, i32 = jnp.float32, jnp.int32
    shape = jax.ShapeDtypeStruct
    pose = view_pose[0]
    camera = jnp.concatenate(
        [jnp.stack([jnp.sin(pose[0]), jnp.cos(pose[0]), jnp.sin(pose[1]), jnp.cos(pose[1])]), pose[2:4]]
    )

    wanted, table, count = pl.pallas_call(
        request_kernel,
        out_shape=[shape((groups, 1, CAP), i32), shape((tiles, slots), i32), shape((tiles,), i32)],
        in_specs=[SMEM, SMEM],
        out_specs=[SMEM, SMEM, SMEM],
        scratch_shapes=[pltpu.SMEM((groups,), i32)],
        name="requests",
    )(tile_blocks[0], tile_order[0])
    asked = lax.all_to_all(wanted, "gs", split_axis=0, concat_axis=0, tiled=True)
    feats = pl.pallas_call(
        project_kernel,
        out_shape=shape((blocks, 16, BLK), f32),
        in_specs=[SMEM, VMEM],
        out_specs=VMEM,
        scratch_shapes=[pltpu.VMEM((blocks, 16, BLK), f32)],
        compiler_params=params_of(24),
        name="project",
    )(camera, gauss_params)
    outgoing = pl.pallas_call(
        pick_kernel,
        out_shape=shape((groups, FEATS, CAP, BLK), f32),
        in_specs=[SMEM, VMEM],
        out_specs=VMEM,
        compiler_params=params_of(16),
        name="pick",
    )(asked, feats)
    arrived = lax.all_to_all(outgoing, "gs", split_axis=0, concat_axis=0, tiled=True)
    image, back = render(table, count, arrived, target_image[0])
    landed = lax.all_to_all(back, "gs", split_axis=0, concat_axis=0, tiled=True)
    own = pl.pallas_call(
        land_kernel,
        out_shape=shape((blocks // 8, FEATS + 1, 8, BLK), f32),
        in_specs=[SMEM, SMEM, VMEM, VMEM],
        out_specs=VMEM,
        scratch_shapes=[pltpu.VMEM((blocks, 16, BLK), f32)],
        compiler_params=params_of(16),
        name="land",
    )(asked, camera, landed, feats)
    others = [
        lax.ppermute(own, "view", [((i + k) % views, i) for i in range(views)]) for k in range(1, views)
    ]
    chunk = 8 * BLK
    wide = pl.BlockSpec((PARAMS, chunk), lambda i: (0, i))
    deep = pl.BlockSpec((1, FEATS + 1, 8, BLK), lambda i: (i, 0, 0, 0))
    new_params, new_first, new_second = pl.pallas_call(
        update_kernel,
        grid=(columns // chunk,),
        out_shape=[shape((PARAMS, columns), f32)] * 3,
        in_specs=[wide] * 3 + [deep] * 4,
        out_specs=[wide] * 3,
        scratch_shapes=[
            pltpu.VMEM((views, FEATS + 1, 8, BLK), f32),
            pltpu.VMEM((8, 16, BLK), f32),
            pltpu.VMEM((8, 16, BLK), f32),
            pltpu.VMEM((views, 64, BLK), f32),
        ],
        compiler_params=params_of(24),
        name="update",
    )(gauss_params, first_moment, second_moment, own, *others)
    return (new_params, new_first, new_second, image[None])


def solution(mesh):
    placed = (
        P(None, "gs"),
        P(None, "gs"),
        P(None, "gs"),
        P("view", None),
        P("view", "gs", None),
        P("view", "gs", None),
        P("view", "gs", None, None),
    )
    return jax.shard_map(
        shards,
        mesh=mesh,
        in_specs=placed,
        out_specs=(P(None, "gs"), P(None, "gs"), P(None, "gs"), P("view", "gs", None, None)),
        check_vma=False,
    )
```

```python
import functools
import math

import jax
import jax.numpy as jnp
from jax import lax
from jax.experimental import pallas as pl
from jax.experimental.pallas import tpu as pltpu
from jax.sharding import PartitionSpec as P

PARAMS = 59
BLK = 128
PIX = 256
FEATS = 9
CAP = 2
ADAM_STEP = 20

beta_one = 0.9
beta_two = 0.999
learn_rate = 0.01
adam_eps = 1e-08
dilation = 0.3
LOG2E = 1.4426950408889634
TINY = 1.1754944e-38
BELOW_ONE = 0.99999994
PROJECT_MB = 56
UPDATE_MB = 24
PROJECT_BLOCKS = 32
UPDATE_BLOCKS = 8

VMEM = pl.BlockSpec(memory_space=pltpu.VMEM)
SMEM = pl.BlockSpec(memory_space=pltpu.SMEM)


def params_of(megabytes):
    return pltpu.CompilerParams(vmem_limit_bytes=megabytes << 20)


def harmonics(x, y, z):
    square_x, square_y, square_z = (x * x, y * y, z * z)
    return [
        0.28209479177387814 + 0.0 * x,
        -0.4886025119029199 * y,
        0.4886025119029199 * z,
        -0.4886025119029199 * x,
        1.0925484305920792 * x * y,
        -1.0925484305920792 * y * z,
        0.31539156525252005 * (2.0 * square_z - square_x - square_y),
        -1.0925484305920792 * x * z,
        0.5462742152960396 * (square_x - square_y),
        -0.5900435899266435 * y * (3.0 * square_x - square_y),
        2.890611442640554 * x * y * z,
        -0.4570457994644658 * y * (4.0 * square_z - square_x - square_y),
        0.3731763325901154 * z * (2.0 * square_z - 3.0 * square_x - 3.0 * square_y),
        -0.4570457994644658 * x * (4.0 * square_z - square_x - square_y),
        1.445305721320277 * z * (square_x - square_y),
        -0.5900435899266435 * x * (square_x - 3.0 * square_y),
    ]


def camera_of(pose_ref):
    yaw, tilt, shift_x, shift_y = [jnp.full((1, BLK), pose_ref[0, k]) for k in range(4)]
    return [jnp.sin(yaw), jnp.cos(yaw), jnp.sin(tilt), jnp.cos(tilt), shift_x, shift_y]


def look_terms(camera):
    sin_yaw, cos_yaw, sin_tilt, cos_tilt = camera[0:4]
    return harmonics(sin_yaw * cos_tilt, -sin_tilt, cos_yaw * cos_tilt)


def axes(camera):
    sin_yaw, cos_yaw, sin_tilt, cos_tilt = camera[0:4]
    return (cos_yaw, -sin_yaw), (sin_yaw * sin_tilt, cos_tilt, cos_yaw * sin_tilt)


def frame(*rows):
    scales = [16.0 * jnp.exp(value) for value in rows[0:3]]
    w, x, y, z = rows[3:7]
    inverse = lax.rsqrt(jnp.maximum(w * w + x * x + y * y + z * z, 1.0))
    w, x, y, z = (w * inverse, x * inverse, y * inverse, z * inverse)
    rotation = (
        (1.0 - 2.0 * (y * y + z * z), 2.0 * (x * y - w * z), 2.0 * (x * z + w * y)),
        (2.0 * (x * y + w * z), 1.0 - 2.0 * (x * x + z * z), 2.0 * (y * z - w * x)),
        (2.0 * (x * z - w * y), 2.0 * (y * z + w * x), 1.0 - 2.0 * (x * x + y * y)),
    )
    return tuple(scales[k] * rotation[r][k] for r in range(3) for k in range(3))


def conic(matrix, camera):
    right, upward = axes(camera)
    first = [right[0] * matrix[k] + right[1] * matrix[6 + k] for k in range(3)]
    second = [
        upward[0] * matrix[k] + upward[1] * matrix[3 + k] + upward[2] * matrix[6 + k]
        for k in range(3)
    ]
    spread_first = first[0] * first[0] + first[1] * first[1] + first[2] * first[2] + dilation
    spread_mixed = first[0] * second[0] + first[1] * second[1] + first[2] * second[2]
    spread_second = second[0] * second[0] + second[1] * second[1] + second[2] * second[2] + dilation
    determinant = spread_first * spread_second - spread_mixed * spread_mixed
    return (spread_second / determinant, -spread_mixed / determinant, spread_first / determinant)


def geometry(rows, camera):
    right, upward = axes(camera)
    across = 16.0 * (right[0] * rows[0] + right[1] * rows[2]) + camera[4]
    downward = 16.0 * (upward[0] * rows[0] + upward[1] * rows[1] + upward[2] * rows[2]) + camera[5]
    return [across, downward, *conic(frame(*rows[3:10]), camera)]


def split(value, parts):
    out = []
    for _ in range(parts - 1):
        high = value.astype(jnp.bfloat16).astype(jnp.float32)
        out.append(high)
        value = value - high
    out.append(value)
    return out


def request_kernel(blocks_ref, order_ref, wanted_ref, table_ref, count_ref):
    tiles, slots = blocks_ref.shape
    holders = wanted_ref.shape[0]
    count = tiles * slots
    by_holder = 6
    by_tile = 4

    def flat(ref):
        return jnp.concatenate([ref[t : t + 1, :] for t in range(tiles)], axis=1)

    def spread(row):
        return jnp.broadcast_to(row, (count, count))

    def add(keep, value, axis):
        return jnp.sum(jnp.where(keep, value, 0.0), axis=axis, keepdims=True)

    def whole(value):
        return value.astype(jnp.int32)

    row = lax.broadcasted_iota(jnp.int32, (count, count), 0)
    lane = lax.broadcasted_iota(jnp.int32, (count, count), 1)
    row_tile, lane_tile = (row >> by_tile, lane >> by_tile)
    block = spread(flat(blocks_ref))
    holder = block >> by_holder
    earlier = whole(add((holder.T == holder) & (row < lane), 1.0, 0))
    slot = spread(jnp.where(block[0:1] >= 0, holder[0:1] * CAP + earlier, -1))
    within = (block - (holder << by_holder) + 1).astype(jnp.float32)
    wanted = [
        whole(add(slot[0:holders] == CAP * row[0:holders] + c, within[0:holders], 1)) - 1
        for c in range(CAP)
    ]
    wanted = jnp.where(lane[0:holders] == 0, wanted[0], wanted[1])
    for h in range(holders):
        wanted_ref[h] = wanted[h : h + 1, 0:CAP]
    filled = add(slot.T == lane, 1.0, 0)
    spare = jnp.max(
        jnp.where(filled > 0.0, 0.0, lane[0:1].astype(jnp.float32)), axis=1, keepdims=True
    )
    place = spread(flat(order_ref) + (lane_tile[0:1] << by_tile)).T
    chosen = add(place == lane, (slot + 1).astype(jnp.float32), 1) - 1.0
    used = jnp.broadcast_to((chosen >= 0.0).astype(jnp.float32), (count, count))
    same = row_tile == lane_tile
    rank = whole(add(same & (lane < row), used.T, 1))
    target = jnp.where(chosen >= 0.0, (row[:, 0:1] & -slots) + rank, -1)
    table_ref[...] = whole(add(target == lane, chosen - spare, 0) + spare)
    count_ref[...] = whole(add(row_tile == lane, used, 0))


def project_kernel(pose_ref, params_ref, feats_ref, turned, seen, weight):
    @pl.when(pl.program_id(0) == 0)
    def _():
        camera = camera_of(pose_ref)
        for k in range(6):
            seen[k : k + 1, :] = camera[k]
        terms = look_terms(camera)
        for c in range(3):
            row = lax.broadcasted_iota(jnp.int32, (24, BLK), 0) - 3
            value = jnp.zeros((24, BLK), jnp.float32)
            for j in range(16):
                value = jnp.where(row == j, terms[j], value)
            weight[c] = value

    camera = [seen[k : k + 1, :] for k in range(6)]
    for j in range(PROJECT_BLOCKS):
        turned[j] = params_ref[0:16, j * BLK : (j + 1) * BLK]
    for j in range(PROJECT_BLOCKS):
        columns = slice(j * BLK, (j + 1) * BLK)
        for c in range(3):
            low = 16 * c + 8
            high = min(low + 24, PARAMS)
            terms = params_ref[low : low + 16, columns] * weight[c, 0:16]
            ends = params_ref[low + 16 : high, columns] * weight[c, 16 : high - low]
            terms = terms[0:8] + terms[8:16]
            if high - low == 24:
                shade = jnp.sum(terms + ends, axis=0, keepdims=True)
            else:
                shade = jnp.sum(terms, axis=0, keepdims=True) + jnp.sum(ends, axis=0, keepdims=True)
            shade = 0.5 + shade
            mask = jnp.where(shade > 0.0, 1.0, jnp.where(shade == 0.0, 0.5, 0.0))
            feats_ref[j, 6 + c : 7 + c, :] = jnp.maximum(shade, 0.0)
            feats_ref[j, 9 + c : 10 + c, :] = mask
    rows = [turned[:, r, :] for r in range(11)]
    opacity = 1.0 / (1.0 + jnp.exp(-rows[10]))
    for r, value in enumerate(geometry(rows, camera) + [opacity]):
        feats_ref[:, r, :] = value


def pick_kernel(asked_ref, feats_ref, out_ref):
    def one(h, _):
        for c in range(CAP):
            block = lax.max(asked_ref[h, 0, c], 0)
            out_ref[h, :, c, :] = feats_ref[block][0:FEATS]
        return 0

    lax.fori_loop(0, out_ref.shape[0], one, 0, unroll=8)


def bands(earlier):
    row = lax.broadcasted_iota(jnp.int32, (4 * BLK, 2 * BLK), 0) % (2 * BLK)
    column = lax.broadcasted_iota(jnp.int32, (4 * BLK, 2 * BLK), 1)
    inside = row < column if earlier else row > column
    return inside.astype(jnp.float32).astype(jnp.bfloat16)


def halves_of(value):
    high = value.astype(jnp.bfloat16)
    low = (value - high.astype(jnp.float32)).astype(jnp.bfloat16)
    return jnp.concatenate([high, low], axis=1)


def sums_by(values, band):
    rows = values[0].shape[0]
    halves = jnp.concatenate([halves_of(value) for value in values], axis=0)
    total = jnp.dot(halves, band[...], preferred_element_type=jnp.float32)
    return [total[rows * h : rows * (h + 1)] for h in range(len(values))]


def twice(value):
    return jnp.concatenate([value, value], axis=1)


def fold(value):
    return jnp.sum(value.reshape(-1, 8, BLK), axis=0)


def render_kernel(
    table_ref,
    count_ref,
    arrived_ref,
    goal_ref,
    image_ref,
    back_ref,
    ranked,
    before,
    after,
    basis,
    *buffers,
):
    my_row = lax.axis_index("gs")
    lanes = tuple(buffers[h::4] for h in range(4))
    tiles = goal_ref.shape[1]
    slots = table_ref.shape[1] // tiles
    before[...] = bands(True)
    after[...] = bands(False)
    pixel = lax.broadcasted_iota(jnp.int32, (PIX, 48), 0)
    place = lax.broadcasted_iota(jnp.int32, (PIX, 48), 1)
    x = (pixel % 16).astype(jnp.float32) - 7.5
    y = (pixel // 16).astype(jnp.float32) - 7.5
    powers = jnp.where((place < 24) & (place % 8 == 0), 1.0, 0.0)
    for k, value in enumerate((x, y, x * x, x * y, y * y)):
        powers = jnp.where((place < 24) & (place % 8 == k + 1), value, powers)
    basis[...] = powers.astype(jnp.bfloat16)
    x = lax.broadcasted_iota(jnp.int32, (16, BLK), 0).astype(jnp.float32) - 7.5
    blank = jnp.zeros((8, PIX), jnp.float32)
    slot_at = lax.broadcasted_iota(jnp.int32, (slots, BLK), 0)
    for _, terms, *_ in lanes:
        terms[...] = jnp.zeros_like(terms)
    counts = [count_ref[0, t] for t in range(tiles)]
    for t in range(tiles):
        rank = jnp.int32(0)
        for s in range(tiles):
            ahead = counts[s] >= counts[t] if s < t else counts[s] > counts[t]
            if s != t:
                rank = rank + ahead.astype(jnp.int32)
        ranked[rank] = t

    def side_by_side(ref, at, j):
        return jnp.concatenate(
            [ref[at, pl.ds(2 * j + k, 1), :].reshape(-1, BLK) for k in range(2)], axis=1
        )

    def local(t, rows):
        u = rows[0] - (16 * t + 8).astype(jnp.float32)
        v = rows[1] - (16 * my_row + 8).astype(jnp.float32)
        return u, v, rows[2], rows[3], rows[4]

    def prepare(t, used, rows, terms):
        for i in range(slots):
            slot = table_ref[0, t * slots + i]
            holder, place = slot // CAP, slot % CAP
            for f in range(FEATS):
                rows[f, i : i + 1, :] = arrived_ref[holder, f, pl.ds(place, 1), :]
        u, v, a, b, d = local(t, rows)
        au, bv = (a * u + b * v, b * u + d * v)
        full = jnp.log2(jnp.maximum(rows[5], TINY)) - (0.5 * LOG2E) * (au * u + bv * v)
        shape = [full, LOG2E * au, LOG2E * bv, (-0.5 * LOG2E) * a, -LOG2E * b, (-0.5 * LOG2E) * d]
        for k, value in enumerate(shape):
            value = jnp.where(slot_at < used, value, -2e4 if k == 0 else 0.0)
            for p, part in enumerate(split(value, 3)):
                terms[8 * p + k] = part
        for k in range(3):
            tint = jnp.where(slot_at < used, rows[6 + k], 0.0)
            rows[6 + k] = tint
            high, mid, low = split(tint, 3)
            for p, part in enumerate((high, high, mid, high, low, mid)):
                terms[24 + 3 * p + k] = part

    def tile_pair(g, _):
        chosen = [ranked[4 * g + h] for h in range(4)]
        used = [count_ref[0, t] for t in chosen]
        pairs = (functools.reduce(lax.max, used) + 1) // 2
        for h, (rows, terms, _, _, shades, _, _) in enumerate(lanes):
            prepare(chosen[h], used[h], rows, terms)
            shades[...] = jnp.zeros_like(shades)

        def forward(j, logs):
            state = []
            for rows, terms, *_ in lanes:
                coefs = side_by_side(terms, slice(None), j).astype(jnp.bfloat16)
                state.append(jnp.dot(basis[...], coefs, preferred_element_type=jnp.float32))
            state = [jnp.minimum(jnp.exp2(value), BELOW_ONE) for value in state]
            losses = [jnp.log2(1.0 - alpha) for alpha in state]
            runs = sums_by(losses, before)
            out = []
            for h, (rows, _, ratios, weights, shades, _, _) in enumerate(lanes):
                alpha, loss, run = state[h], losses[h], runs[h]
                ratios[j] = alpha * jnp.exp2(-loss)
                weight = alpha * jnp.exp2(run + twice(logs[h]))
                weights[j] = weight
                tints = side_by_side(rows, slice(6, 9), j)
                for c in range(3):
                    shade = weight * tints[c : c + 1]
                    shades[c] += shade[:, 0:BLK] + shade[:, BLK:]
                last = run[:, 2 * BLK - 1 :] + loss[:, 2 * BLK - 1 :]
                out.append(logs[h] + jnp.broadcast_to(last, (PIX, BLK)))
            return tuple(out)

        still = jnp.zeros((PIX, BLK), jnp.float32)
        lax.fori_loop(0, pairs, forward, (still,) * 4)
        lane = lax.broadcasted_iota(jnp.int32, (PIX, BLK), 1)
        pulled = []
        for h, (_, _, _, _, shades, pulls, _) in enumerate(lanes):
            columns = jnp.zeros((PIX, BLK), jnp.float32)
            for c in range(3):
                columns = jnp.where(lane == c, jnp.sum(shades[c], axis=1, keepdims=True), columns)
            image = columns.T[0:3]
            at = pl.ds(chosen[h], 1)
            for c in range(3):
                image_ref[c, at, :] = image[c : c + 1]
            pull = image - jnp.concatenate([goal_ref[c, at, :] for c in range(3)], axis=0)
            high, mid, low = split(pull, 3)
            turned = jnp.concatenate(
                [blank] * 3 + [high, mid, high, low, high, mid, pull, blank[0:3]], axis=0
            ).T
            for c in range(3):
                pulls[c] = jnp.broadcast_to(turned[:, 42 + c : 43 + c], (PIX, BLK))
            pulled.append(turned.astype(jnp.bfloat16))

        def backward(step, later):
            j = pairs - 1 - step
            reaches = []
            for h, (_, terms, _, weights, *_) in enumerate(lanes):
                coefs = side_by_side(terms, slice(None), j).astype(jnp.bfloat16)
                reaches.append(
                    jnp.dot(pulled[h], coefs, preferred_element_type=jnp.float32) * weights[j]
                )
            behinds = sums_by(reaches, after)
            out = []
            for h, (_, _, ratios, weights, _, pulls, sums) in enumerate(lanes):
                reach, behind, weight = reaches[h], behinds[h], weights[j]
                push = reach - (behind + twice(later[h])) * ratios[j]
                for k in range(2):
                    at = slice(BLK * k, BLK * (k + 1))
                    slot = pl.ds(2 * j + k, 1)
                    part = push[:, at].reshape(16, 16, BLK)
                    plain, tilted, bent = (None, None, None)
                    for n in range(8):
                        y = 7.5 - n
                        even, odd = (part[15 - n] + part[n], y * (part[15 - n] - part[n]))
                        square = (y * y) * even
                        plain = even if n == 0 else plain + even
                        tilted = odd if n == 0 else tilted + odd
                        bent = square if n == 0 else bent + square
                    values = (plain, x * plain, tilted, x * x * plain, x * tilted, bent)
                    for f, value in enumerate(values):
                        sums[f, slot] = (value[0:8] + value[8:16]).reshape(1, 8, BLK)
                    for c in range(3):
                        sums[6 + c, slot] = fold(weight[:, at] * pulls[c]).reshape(1, 8, BLK)
                out.append(
                    later[h] + jnp.broadcast_to(behind[:, 0:1] + reach[:, 0:1], (PIX, BLK))
                )
            return tuple(out)

        lax.fori_loop(0, pairs, backward, (still,) * 4)
        for h, (rows, _, _, _, _, _, sums) in enumerate(lanes):
            t = chosen[h]
            u, v, a, b, d = local(t, rows)
            m0, mx, my, mxx, mxy, myy, red, green, blue = [
                sum(sums[f, :, s, :] for s in range(8)) for f in range(FEATS)
            ]
            cx, cy = (mx - u * m0, my - v * m0)
            rows[0] = a * cx + b * cy
            rows[1] = b * cx + d * cy
            rows[2] = -0.5 * (mxx - u * (mx + cx))
            rows[3] = -(mxy - u * my - v * cx)
            rows[4] = -0.5 * (myy - v * (my + cy))
            for f, value in ((5, m0), (6, red), (7, green), (8, blue)):
                rows[f] = value

            for i in range(slots):
                slot = table_ref[0, t * slots + i]
                holder, place = slot // CAP, slot % CAP
                for f in range(FEATS):
                    back_ref[holder, f, pl.ds(place, 1), :] = rows[f, i : i + 1, :]
        return 0

    lax.fori_loop(0, tiles // 4, tile_pair, 0)


def render(table, count, arrived, goal):
    tiles = goal.shape[1]
    slots = table.shape[1] // tiles
    groups = arrived.shape[0]
    f32 = jnp.float32
    shape = jax.ShapeDtypeStruct
    return pl.pallas_call(
        render_kernel,
        out_shape=[shape((3, tiles, PIX), f32), shape((groups, FEATS, CAP, BLK), f32)],
        in_specs=[SMEM, SMEM, VMEM, VMEM],
        out_specs=[VMEM, VMEM],
        scratch_shapes=[
            pltpu.SMEM((tiles,), jnp.int32),
            pltpu.VMEM((4 * BLK, 2 * BLK), jnp.bfloat16),
            pltpu.VMEM((4 * BLK, 2 * BLK), jnp.bfloat16),
            pltpu.VMEM((PIX, 48), jnp.bfloat16),
        ]
        + [
            pltpu.VMEM(dims, f32)
            for dims in (
                (FEATS, slots, BLK),
                (48, slots, BLK),
                (slots // 2, PIX, 2 * BLK),
                (slots // 2, PIX, 2 * BLK),
                (3, PIX, BLK),
                (3, PIX, BLK),
                (FEATS, slots, 8, BLK),
            )
            for _ in range(4)
        ],
        compiler_params=params_of(40),
        name="render",
    )(table, count, arrived, goal)


def land_kernel(asked_ref, pose_ref, landed_ref, feats_ref, out_ref, total):
    total[...] = jnp.zeros_like(total)
    groups = out_ref.shape[0]

    def one(h, _):
        for c in range(CAP):
            block = asked_ref[h, 0, c]
            block = jnp.where(block < 0, 8 * groups, block)
            total[block, 0:FEATS, :] = total[block, 0:FEATS, :] + landed_ref[h, :, c, :]
        return 0

    lax.fori_loop(0, landed_ref.shape[0], one, 0, unroll=8)
    place = lax.broadcasted_iota(jnp.int32, (8, BLK), 0)
    shown = jnp.zeros((8, BLK), jnp.float32)
    for k, value in enumerate(camera_of(pose_ref)):
        shown = jnp.where(place == k, value, shown)
    for g in range(groups):
        for f in range(FEATS):
            value = total[8 * g : 8 * g + 8, f, :]
            if f >= 6:
                value = value * feats_ref[8 * g : 8 * g + 8, f + 3, :]
            out_ref[g, f] = value
        out_ref[g, FEATS] = shown


def adam(weights_in, moment_one, moment_two, gradient):
    new_first = beta_one * moment_one + (1.0 - beta_one) * gradient
    new_second = beta_two * moment_two + (1.0 - beta_two) * gradient * gradient
    step_size = learn_rate / (1.0 - beta_one**ADAM_STEP)
    new_params = weights_in - step_size * new_first / (
        jnp.sqrt(new_second / (1.0 - beta_two**ADAM_STEP)) + adam_eps
    )
    return (new_params, new_first, new_second)


def update_kernel(
    params_ref, first_ref, second_ref, own_ref, next_ref, low_ref, high_ref, last_ref,
    new_params_ref, new_first_ref, new_second_ref, pulls, turned, shades, waves, ready, sent,
):
    me = lax.axis_index("view")
    views = 4
    outs = (new_params_ref, new_first_ref, new_second_ref)
    groups = own_ref.shape[0]
    span = UPDATE_BLOCKS // 8
    steps = groups // span
    chunk = UPDATE_BLOCKS * BLK
    for v in range(views):
        from_one = [own_ref, next_ref, None, last_ref]
        pulls[(me + v) % views] = (
            jnp.concatenate([low_ref[...], high_ref[...]], axis=0) if v == 2 else from_one[v][...]
        )
    for v in range(views):
        terms = look_terms([pulls[v, 0, FEATS, k : k + 1, :] for k in range(6)])
        for k in range(8):
            row = lax.broadcasted_iota(jnp.int32, (8, BLK), 0) + (8 * k - 11)
            wave = jnp.zeros((8, BLK), jnp.float32)
            for j in range(16):
                wave = jnp.where((row >= 0) & (row % 16 == j), terms[j], wave)
            waves[v, 8 * k : 8 * k + 8, :] = wave

    def plus(left, right):
        return right if left is None else [p + q for p, q in zip(left, right)]

    def copies(step):
        slot = step % 2
        at = slice(step * chunk, (step + 1) * chunk)
        return [
            pltpu.make_async_copy(ready.at[slot, n], outs[n].at[:, at], sent.at[slot, n])
            for n in range(3)
        ]

    row_in = lax.broadcasted_iota(jnp.int32, (8, BLK), 0)
    for step in range(steps):
        base = step * chunk
        for j in range(UPDATE_BLOCKS):
            turned[j] = params_ref[0:16, base + j * BLK : base + (j + 1) * BLK]

        def of(r):
            return turned[:, r, :].reshape(span, 8, BLK)

        rows = [of(r) for r in range(11)]
        opacity = 1.0 / (1.0 + jnp.exp(-rows[10]))
        matrix, pull_frame = jax.vjp(frame, *rows[3:10])
        centre, bent = (None, None)
        for v in range(views):
            camera = [pulls[v, 0, FEATS, k : k + 1, :] for k in range(6)]
            right, upward = axes(camera)
            seen = [pulls[v, step * span : (step + 1) * span, f] for f in range(FEATS)]
            across, downward = (16.0 * seen[0], 16.0 * seen[1])
            moved = [
                right[0] * across + upward[0] * downward,
                upward[1] * downward,
                right[1] * across + upward[2] * downward,
                seen[5],
            ]
            centre = plus(centre, moved)
            _, pull_conic = jax.vjp(lambda m: conic(m, camera), matrix)
            bent = plus(bent, pull_conic(tuple(seen[2:5]))[0])
            for c in range(3):
                shades[:, 3 * v + c, :] = seen[6 + c].reshape(UPDATE_BLOCKS, BLK)
        total = centre[0:3] + list(pull_frame(tuple(bent))) + [centre[3] * (1.0 - opacity)]
        for r in range(11):
            turned[:, r, :] = total[r].reshape(UPDATE_BLOCKS, BLK)
        if step >= 2:
            for copy in copies(step - 2):
                copy.wait()
        slot = step % 2
        for j in range(UPDATE_BLOCKS):
            columns = slice(base + j * BLK, base + (j + 1) * BLK)
            for k in range(8):
                gradient = None
                if k > 0:
                    first = (8 * k - 11) // 16 if k > 1 else 0
                    last = min((8 * k + 7 - 11) // 16, 2)
                    for v in range(views):
                        tint = shades[j, 3 * v + first : 3 * v + first + 1, :]
                        if last != first:
                            tint = jnp.where(
                                row_in + (8 * k - 11) < 16 * last,
                                tint,
                                shades[j, 3 * v + last : 3 * v + last + 1, :],
                            )
                        term = waves[v, 8 * k : 8 * k + 8, :] * tint
                        gradient = term if gradient is None else gradient + term
                if k == 0:
                    gradient = turned[j, 0:8, :]
                if k == 1:
                    gradient = jnp.where(row_in < 3, turned[j, 8:16, :], gradient)
                height = min(8, PARAMS - 8 * k)
                at = (slice(8 * k, 8 * k + height), columns)
                values = adam(params_ref[at], first_ref[at], second_ref[at], gradient[0:height])
                for n in range(3):
                    ready[slot, n, 8 * k : 8 * k + height, j * BLK : (j + 1) * BLK] = values[n]
        for copy in copies(step):
            copy.start()
    for step in range(max(steps - 2, 0), steps):
        for copy in copies(step):
            copy.wait()


def project(view_pose, gauss_params):
    columns = gauss_params.shape[1]
    blocks = columns // BLK
    f32 = jnp.float32
    shape = jax.ShapeDtypeStruct
    chunk = PROJECT_BLOCKS * BLK
    wide = pl.BlockSpec((PARAMS, chunk), lambda i: (0, i))
    steps = columns // chunk
    return pl.pallas_call(
        project_kernel,
        grid=(steps,),
        out_shape=shape((blocks, 16, BLK), f32),
        in_specs=[SMEM, wide],
        out_specs=pl.BlockSpec((PROJECT_BLOCKS, 16, BLK), lambda i: (i, 0, 0)),
        scratch_shapes=[
            pltpu.VMEM((PROJECT_BLOCKS, 16, BLK), f32),
            pltpu.VMEM((8, BLK), f32),
            pltpu.VMEM((3, 24, BLK), f32),
        ],
        compiler_params=params_of(PROJECT_MB),
        name="project",
    )(view_pose, gauss_params)


def update(gauss_params, first_moment, second_moment, own, after, low, high, prior):
    groups = own.shape[0]
    f32 = jnp.float32
    views = 4
    chunk = UPDATE_BLOCKS * BLK
    return pl.pallas_call(
        update_kernel,
        out_shape=[jax.ShapeDtypeStruct(gauss_params.shape, f32)] * 3,
        in_specs=[VMEM] * 8,
        out_specs=[pl.BlockSpec(memory_space=pl.ANY)] * 3,
        scratch_shapes=[
            pltpu.VMEM((views, groups, FEATS + 1, 8, BLK), f32),
            pltpu.VMEM((UPDATE_BLOCKS, 16, BLK), f32),
            pltpu.VMEM((UPDATE_BLOCKS, 16, BLK), f32),
            pltpu.VMEM((views, 64, BLK), f32),
            pltpu.VMEM((2, 3, PARAMS, chunk), f32),
            pltpu.SemaphoreType.DMA((2, 3)),
        ],
        compiler_params=params_of(UPDATE_MB),
        name="update",
    )(gauss_params, first_moment, second_moment, own, after, low, high, prior)


def shards(
    gauss_params, first_moment, second_moment, view_pose, tile_blocks, tile_order, target_image
):
    groups = lax.axis_size("gs")
    views = lax.axis_size("view")
    columns = gauss_params.shape[1]
    blocks = columns // BLK
    tiles, slots = tile_blocks.shape[1:]
    f32, i32 = jnp.float32, jnp.int32
    shape = jax.ShapeDtypeStruct
    steps = blocks // 8

    wanted, table, count = pl.pallas_call(
        request_kernel,
        out_shape=[shape((groups, 1, CAP), i32)] + [shape((1, tiles * slots), i32)] * 2,
        in_specs=[VMEM, VMEM],
        out_specs=[VMEM, VMEM, VMEM],
        name="requests",
    )(tile_blocks[0], tile_order[0])
    asked = lax.all_to_all(wanted, "gs", split_axis=0, concat_axis=0, tiled=True)
    feats = project(view_pose, gauss_params)
    outgoing = pl.pallas_call(
        pick_kernel,
        out_shape=shape((groups, FEATS, CAP, BLK), f32),
        in_specs=[SMEM, VMEM],
        out_specs=VMEM,
        compiler_params=params_of(16),
        name="pick",
    )(asked, feats)
    arrived = lax.all_to_all(outgoing, "gs", split_axis=0, concat_axis=0, tiled=True)
    image, back = render(table, count, arrived, jnp.transpose(target_image[0], (1, 0, 2)))
    landed = lax.all_to_all(back, "gs", split_axis=0, concat_axis=0, tiled=True)
    own = pl.pallas_call(
        land_kernel,
        out_shape=shape((blocks // 8, FEATS + 1, 8, BLK), f32),
        in_specs=[SMEM, SMEM, VMEM, VMEM],
        out_specs=VMEM,
        scratch_shapes=[pltpu.VMEM((blocks + 1, 16, BLK), f32)],
        compiler_params=params_of(16),
        name="land",
    )(asked, view_pose, landed, feats)

    def from_next(value, k):
        return lax.ppermute(value, "view", [((i + k) % views, i) for i in range(views)])

    half = steps // 2
    after = from_next(own, 1)
    prior = from_next(own, views - 1)
    low = from_next(after[:half], 1)
    high = from_next(prior[half:], views - 1)
    new_params, new_first, new_second = update(
        gauss_params, first_moment, second_moment, own, after, low, high, prior
    )
    return (new_params, new_first, new_second, jnp.transpose(image, (1, 0, 2))[None])


def solution(mesh):
    placed = (
        P(None, "gs"),
        P(None, "gs"),
        P(None, "gs"),
        P("view", None),
        P("view", "gs", None),
        P("view", "gs", None),
        P("view", "gs", None, None),
    )
    return jax.shard_map(
        shards,
        mesh=mesh,
        in_specs=placed,
        out_specs=(P(None, "gs"), P(None, "gs"), P(None, "gs"), P("view", "gs", None, None)),
        check_vma=False,
    )
```

```python
import functools
import math

import jax
import jax.numpy as jnp
from jax import lax
from jax.experimental import pallas as pl
from jax.experimental.pallas import tpu as pltpu
from jax.sharding import PartitionSpec as P

PARAMS = 59
BLK = 128
PIX = 256
FEATS = 9
CAP = 2
ADAM_STEP = 20

beta_one = 0.9
beta_two = 0.999
learn_rate = 0.01
adam_eps = 1e-08
dilation = 0.3
LOG2E = 1.4426950408889634
TINY = 1.1754944e-38
BELOW_ONE = 0.99999994
PROJECT_MB = 24
UPDATE_MB = 24
PROJECT_BLOCKS = 32
ROWS = 64
HALF = 4

VMEM = pl.BlockSpec(memory_space=pltpu.VMEM)
SMEM = pl.BlockSpec(memory_space=pltpu.SMEM)


def params_of(megabytes):
    return pltpu.CompilerParams(vmem_limit_bytes=megabytes << 20)


def harmonics(x, y, z):
    square_x, square_y, square_z = (x * x, y * y, z * z)
    return [
        0.28209479177387814 + 0.0 * x,
        -0.4886025119029199 * y,
        0.4886025119029199 * z,
        -0.4886025119029199 * x,
        1.0925484305920792 * x * y,
        -1.0925484305920792 * y * z,
        0.31539156525252005 * (2.0 * square_z - square_x - square_y),
        -1.0925484305920792 * x * z,
        0.5462742152960396 * (square_x - square_y),
        -0.5900435899266435 * y * (3.0 * square_x - square_y),
        2.890611442640554 * x * y * z,
        -0.4570457994644658 * y * (4.0 * square_z - square_x - square_y),
        0.3731763325901154 * z * (2.0 * square_z - 3.0 * square_x - 3.0 * square_y),
        -0.4570457994644658 * x * (4.0 * square_z - square_x - square_y),
        1.445305721320277 * z * (square_x - square_y),
        -0.5900435899266435 * x * (square_x - 3.0 * square_y),
    ]


def camera_of(pose_ref):
    yaw, tilt, shift_x, shift_y = [jnp.full((1, BLK), pose_ref[0, k]) for k in range(4)]
    return [jnp.sin(yaw), jnp.cos(yaw), jnp.sin(tilt), jnp.cos(tilt), shift_x, shift_y]


def look_terms(camera):
    sin_yaw, cos_yaw, sin_tilt, cos_tilt = camera[0:4]
    return harmonics(sin_yaw * cos_tilt, -sin_tilt, cos_yaw * cos_tilt)


def axes(camera):
    sin_yaw, cos_yaw, sin_tilt, cos_tilt = camera[0:4]
    return (cos_yaw, -sin_yaw), (sin_yaw * sin_tilt, cos_tilt, cos_yaw * sin_tilt)


def frame(*rows):
    scales = [16.0 * jnp.exp(value) for value in rows[0:3]]
    w, x, y, z = rows[3:7]
    inverse = lax.rsqrt(jnp.maximum(w * w + x * x + y * y + z * z, 1.0))
    w, x, y, z = (w * inverse, x * inverse, y * inverse, z * inverse)
    rotation = (
        (1.0 - 2.0 * (y * y + z * z), 2.0 * (x * y - w * z), 2.0 * (x * z + w * y)),
        (2.0 * (x * y + w * z), 1.0 - 2.0 * (x * x + z * z), 2.0 * (y * z - w * x)),
        (2.0 * (x * z - w * y), 2.0 * (y * z + w * x), 1.0 - 2.0 * (x * x + y * y)),
    )
    return tuple(scales[k] * rotation[r][k] for r in range(3) for k in range(3))


def spreads(matrix, camera):
    right, upward = axes(camera)
    first = [right[0] * matrix[k] + right[1] * matrix[6 + k] for k in range(3)]
    second = [
        upward[0] * matrix[k] + upward[1] * matrix[3 + k] + upward[2] * matrix[6 + k]
        for k in range(3)
    ]
    spread_first = first[0] * first[0] + first[1] * first[1] + first[2] * first[2] + dilation
    spread_mixed = first[0] * second[0] + first[1] * second[1] + first[2] * second[2]
    spread_second = second[0] * second[0] + second[1] * second[1] + second[2] * second[2] + dilation
    determinant = spread_first * spread_second - spread_mixed * spread_mixed
    return first, second, spread_first, spread_mixed, spread_second, determinant


def conic(matrix, camera):
    _, _, spread_first, spread_mixed, spread_second, determinant = spreads(matrix, camera)
    return (spread_second / determinant, -spread_mixed / determinant, spread_first / determinant)


def conic_pull(matrix, camera, pulls):
    right, upward = axes(camera)
    first, second, spread_first, spread_mixed, spread_second, determinant = spreads(matrix, camera)
    inverse = 1.0 / determinant
    pull_a, pull_b, pull_c = [value * inverse for value in pulls]
    shrink = (pull_b * spread_mixed - pull_a * spread_second - pull_c * spread_first) * inverse
    to_first = 2.0 * (pull_c + shrink * spread_second)
    to_second = 2.0 * (pull_a + shrink * spread_first)
    to_mixed = -pull_b - 2.0 * (shrink * spread_mixed)
    on_first = [to_first * p + to_mixed * q for p, q in zip(first, second)]
    on_second = [to_second * q + to_mixed * p for p, q in zip(first, second)]
    return (
        [right[0] * p + upward[0] * q for p, q in zip(on_first, on_second)]
        + [upward[1] * q for q in on_second]
        + [right[1] * p + upward[2] * q for p, q in zip(on_first, on_second)]
    )


def geometry(rows, camera):
    right, upward = axes(camera)
    across = 16.0 * (right[0] * rows[0] + right[1] * rows[2]) + camera[4]
    downward = 16.0 * (upward[0] * rows[0] + upward[1] * rows[1] + upward[2] * rows[2]) + camera[5]
    return [across, downward, *conic(frame(*rows[3:10]), camera)]


def split(value, parts):
    out = []
    for _ in range(parts - 1):
        high = value.astype(jnp.bfloat16).astype(jnp.float32)
        out.append(high)
        value = value - high
    out.append(value)
    return out


def request_kernel(blocks_ref, order_ref, wanted_ref, table_ref, count_ref):
    tiles, slots = blocks_ref.shape
    holders = wanted_ref.shape[0]
    count = tiles * slots
    by_holder = 6
    by_tile = 4

    def flat(ref):
        return jnp.concatenate([ref[t : t + 1, :] for t in range(tiles)], axis=1)

    def spread(row):
        return jnp.broadcast_to(row, (count, count))

    def add(keep, value, axis):
        return jnp.sum(jnp.where(keep, value, 0.0), axis=axis, keepdims=True)

    def whole(value):
        return value.astype(jnp.int32)

    row = lax.broadcasted_iota(jnp.int32, (count, count), 0)
    lane = lax.broadcasted_iota(jnp.int32, (count, count), 1)
    row_tile, lane_tile = (row >> by_tile, lane >> by_tile)
    block = spread(flat(blocks_ref))
    holder = block >> by_holder
    earlier = whole(add((holder.T == holder) & (row < lane), 1.0, 0))
    slot = spread(jnp.where(block[0:1] >= 0, holder[0:1] * CAP + earlier, -1))
    within = (block - (holder << by_holder) + 1).astype(jnp.float32)
    wanted = [
        whole(add(slot[0:holders] == CAP * row[0:holders] + c, within[0:holders], 1)) - 1
        for c in range(CAP)
    ]
    wanted = jnp.where(lane[0:holders] == 0, wanted[0], wanted[1])
    for h in range(holders):
        wanted_ref[h] = wanted[h : h + 1, 0:CAP]
    filled = add(slot.T == lane, 1.0, 0)
    spare = jnp.max(
        jnp.where(filled > 0.0, 0.0, lane[0:1].astype(jnp.float32)), axis=1, keepdims=True
    )
    place = spread(flat(order_ref) + (lane_tile[0:1] << by_tile)).T
    chosen = add(place == lane, (slot + 1).astype(jnp.float32), 1) - 1.0
    used = jnp.broadcast_to((chosen >= 0.0).astype(jnp.float32), (count, count))
    same = row_tile == lane_tile
    rank = whole(add(same & (lane < row), used.T, 1))
    target = jnp.where(chosen >= 0.0, (row[:, 0:1] & -slots) + rank, -1)
    table_ref[...] = whole(add(target == lane, chosen - spare, 0) + spare)
    count_ref[...] = whole(add(row_tile == lane, used, 0))


def project_kernel(pose_ref, params_ref, feats_ref, turned, seen, weight):
    @pl.when(pl.program_id(0) == 0)
    def _():
        camera = camera_of(pose_ref)
        for k in range(6):
            seen[k : k + 1, :] = camera[k]
        terms = look_terms(camera)
        for c in range(3):
            row = lax.broadcasted_iota(jnp.int32, (24, BLK), 0) - 3
            value = jnp.zeros((24, BLK), jnp.float32)
            for j in range(16):
                value = jnp.where(row == j, terms[j], value)
            weight[c] = value

    camera = [seen[k : k + 1, :] for k in range(6)]
    for j in range(PROJECT_BLOCKS):
        turned[j] = params_ref[0:16, j * BLK : (j + 1) * BLK]
    for j in range(PROJECT_BLOCKS):
        columns = slice(j * BLK, (j + 1) * BLK)
        for c in range(3):
            low = 16 * c + 8
            high = min(low + 24, PARAMS)
            terms = params_ref[low : low + 16, columns] * weight[c, 0:16]
            ends = params_ref[low + 16 : high, columns] * weight[c, 16 : high - low]
            terms = terms[0:8] + terms[8:16]
            if high - low == 24:
                shade = jnp.sum(terms + ends, axis=0, keepdims=True)
            else:
                shade = jnp.sum(terms, axis=0, keepdims=True) + jnp.sum(ends, axis=0, keepdims=True)
            shade = 0.5 + shade
            mask = jnp.where(shade > 0.0, 1.0, jnp.where(shade == 0.0, 0.5, 0.0))
            feats_ref[j, 6 + c : 7 + c, :] = jnp.maximum(shade, 0.0)
            feats_ref[j, 9 + c : 10 + c, :] = mask
    rows = [turned[:, r, :] for r in range(11)]
    opacity = 1.0 / (1.0 + jnp.exp(-rows[10]))
    for r, value in enumerate(geometry(rows, camera) + [opacity]):
        feats_ref[:, r, :] = value


def pick_kernel(asked_ref, feats_ref, out_ref):
    def one(h, _):
        for c in range(CAP):
            block = lax.max(asked_ref[h, 0, c], 0)
            out_ref[h, :, c, :] = feats_ref[block][0:FEATS]
        return 0

    lax.fori_loop(0, out_ref.shape[0], one, 0, unroll=8)


def bands(earlier):
    row = lax.broadcasted_iota(jnp.int32, (4 * BLK, 2 * BLK), 0) % (2 * BLK)
    column = lax.broadcasted_iota(jnp.int32, (4 * BLK, 2 * BLK), 1)
    inside = row < column if earlier else row > column
    return inside.astype(jnp.float32).astype(jnp.bfloat16)


def halves_of(value):
    high = value.astype(jnp.bfloat16)
    low = (value - high.astype(jnp.float32)).astype(jnp.bfloat16)
    return jnp.concatenate([high, low], axis=1)


def twice(value):
    return jnp.concatenate([value, value], axis=1)


def render_kernel(
    table_ref,
    count_ref,
    arrived_ref,
    goal_ref,
    image_ref,
    back_ref,
    ranked,
    before,
    after,
    basis,
    *buffers,
):
    my_row = lax.axis_index("gs")
    lanes = tuple(buffers[h::4] for h in range(4))
    tiles = goal_ref.shape[1]
    slots = table_ref.shape[1] // tiles
    before[...] = bands(True)
    after[...] = bands(False)
    pixel = lax.broadcasted_iota(jnp.int32, (PIX, 48), 0)
    place = lax.broadcasted_iota(jnp.int32, (PIX, 48), 1)
    x = (pixel % 16).astype(jnp.float32) - 7.5
    y = (pixel // 16).astype(jnp.float32) - 7.5
    powers = jnp.where((place < 24) & (place % 8 == 0), 1.0, 0.0)
    for k, value in enumerate((x, y, x * x, x * y, y * y)):
        powers = jnp.where((place < 24) & (place % 8 == k + 1), value, powers)
    basis[...] = powers.astype(jnp.bfloat16)
    x = lax.broadcasted_iota(jnp.int32, (16, 2 * BLK), 0).astype(jnp.float32) - 7.5
    blank = jnp.zeros((8, PIX), jnp.float32)
    slot_at = lax.broadcasted_iota(jnp.int32, (slots, BLK), 0)
    for _, terms, *_ in lanes:
        terms[...] = jnp.zeros_like(terms)
    counts = [count_ref[0, t] for t in range(tiles)]
    for t in range(tiles):
        rank = jnp.int32(0)
        for s in range(tiles):
            ahead = counts[s] >= counts[t] if s < t else counts[s] > counts[t]
            if s != t:
                rank = rank + ahead.astype(jnp.int32)
        ranked[rank] = t

    def side_by_side(ref, at, j):
        return jnp.concatenate(
            [ref[at, pl.ds(2 * j + k, 1), :].reshape(-1, BLK) for k in range(2)], axis=1
        )

    def local(t, rows):
        u = rows[0] - (16 * t + 8).astype(jnp.float32)
        v = rows[1] - (16 * my_row + 8).astype(jnp.float32)
        return u, v, rows[2], rows[3], rows[4]

    def prepare(t, used, rows, terms):
        for i in range(slots):
            slot = table_ref[0, t * slots + i]
            holder, place = slot // CAP, slot % CAP
            for f in range(FEATS):
                rows[f, i : i + 1, :] = arrived_ref[holder, f, pl.ds(place, 1), :]
        u, v, a, b, d = local(t, rows)
        au, bv = (a * u + b * v, b * u + d * v)
        full = jnp.log2(jnp.maximum(rows[5], TINY)) - (0.5 * LOG2E) * (au * u + bv * v)
        shape = [full, LOG2E * au, LOG2E * bv, (-0.5 * LOG2E) * a, -LOG2E * b, (-0.5 * LOG2E) * d]
        for k, value in enumerate(shape):
            value = jnp.where(slot_at < used, value, -2e4 if k == 0 else 0.0)
            for p, part in enumerate(split(value, 3)):
                terms[8 * p + k] = part
        for k in range(3):
            tint = jnp.where(slot_at < used, rows[6 + k], 0.0)
            rows[6 + k] = tint
            high, mid, low = split(tint, 3)
            for p, part in enumerate((high, high, mid, high, low, mid)):
                terms[24 + 3 * p + k] = part

    def tile_pair(g, _):
        chosen = [ranked[4 * g + h] for h in range(4)]
        used = [count_ref[0, t] for t in chosen]
        pairs = (functools.reduce(lax.max, used) + 1) // 2
        for h, (rows, terms, _, _, shades, _, _) in enumerate(lanes):
            prepare(chosen[h], used[h], rows, terms)
            shades[...] = jnp.zeros_like(shades)

        def forward(j, logs):
            state = []
            for rows, terms, *_ in lanes:
                coefs = side_by_side(terms, slice(None), j).astype(jnp.bfloat16)
                state.append(jnp.dot(basis[...], coefs, preferred_element_type=jnp.float32))
            alphas, losses, halves = ([], [], [])
            for h, (_, _, ratios, *_) in enumerate(lanes):
                for r in range(0, PIX, ROWS):
                    alpha = jnp.minimum(jnp.exp2(state[h][r : r + ROWS]), BELOW_ONE)
                    loss = jnp.log2(1.0 - alpha)
                    ratios[j, r : r + ROWS] = alpha * jnp.exp2(-loss)
                    alphas.append(alpha)
                    losses.append(loss)
                    halves.append(halves_of(loss))
            run = jnp.dot(
                jnp.concatenate(halves, axis=0), before[...], preferred_element_type=jnp.float32
            )
            out = []
            for h, (rows, _, _, weights, shades, _, _) in enumerate(lanes):
                tints = side_by_side(rows, slice(6, 9), j)
                lasts = []
                for r in range(0, PIX, ROWS):
                    n = (h * PIX + r) // ROWS
                    mine = run[h * PIX + r : h * PIX + r + ROWS]
                    log = logs[h][r : r + ROWS]
                    weight = alphas[n] * jnp.exp2(mine + twice(log))
                    weights[j, r : r + ROWS] = weight
                    for c in range(3):
                        shade = weight * tints[c : c + 1]
                        shades[c, r : r + ROWS] += shade[:, 0:BLK] + shade[:, BLK:]
                    last = mine[:, 2 * BLK - 1 :] + losses[n][:, 2 * BLK - 1 :]
                    lasts.append(log + jnp.broadcast_to(last, (ROWS, BLK)))
                out.append(jnp.concatenate(lasts, axis=0))
            return tuple(out)

        still = jnp.zeros((PIX, BLK), jnp.float32)
        lax.fori_loop(0, pairs, forward, (still,) * 4)
        lane = lax.broadcasted_iota(jnp.int32, (PIX, BLK), 1)
        pulled = []
        for h, (_, _, _, _, shades, pulls, _) in enumerate(lanes):
            columns = jnp.zeros((PIX, BLK), jnp.float32)
            for c in range(3):
                columns = jnp.where(lane == c, jnp.sum(shades[c], axis=1, keepdims=True), columns)
            image = columns.T[0:3]
            at = pl.ds(chosen[h], 1)
            for c in range(3):
                image_ref[c, at, :] = image[c : c + 1]
            pull = image - jnp.concatenate([goal_ref[c, at, :] for c in range(3)], axis=0)
            high, mid, low = split(pull, 3)
            turned = jnp.concatenate(
                [blank] * 3 + [high, mid, high, low, high, mid, pull, blank[0:3]], axis=0
            ).T
            for c in range(3):
                pulls[c] = jnp.broadcast_to(turned[:, 42 + c : 43 + c], (PIX, BLK))
            pulled.append(turned.astype(jnp.bfloat16))

        def backward(step, later):
            j = pairs - 1 - step
            reaches, halves = ([], [])
            for h, (_, terms, _, weights, *_) in enumerate(lanes):
                coefs = side_by_side(terms, slice(None), j).astype(jnp.bfloat16)
                pull = jnp.dot(pulled[h], coefs, preferred_element_type=jnp.float32)
                for r in range(0, PIX, 16):
                    reach = pull[r : r + 16] * weights[j, r : r + 16]
                    reaches.append(reach)
                    halves.append(halves_of(reach))
            behinds = jnp.dot(
                jnp.concatenate(halves, axis=0), after[...], preferred_element_type=jnp.float32
            )
            out = []
            for h, (_, _, ratios, weights, _, pulls, sums) in enumerate(lanes):
                plain, tilted, bent = (None, None, None)
                tints = [None] * 3
                lasts = [None] * 16
                for n in range(8):
                    pair = []
                    for m in (n, 15 - n):
                        at = slice(16 * m, 16 * m + 16)
                        reach = reaches[16 * h + m]
                        behind = behinds[h * PIX + 16 * m : h * PIX + 16 * m + 16]
                        log = later[h][at]
                        pair.append(reach - (behind + twice(log)) * ratios[j, at])
                        last = jnp.broadcast_to(behind[:, 0:1] + reach[:, 0:1], (16, BLK))
                        lasts[m] = log + last
                        weight = weights[j, at]
                        for c in range(3):
                            tint = weight * twice(pulls[c, at])
                            tint = tint[0:8] + tint[8:16]
                            tints[c] = tint if tints[c] is None else tints[c] + tint
                    y = 7.5 - n
                    even, odd = (pair[1] + pair[0], y * (pair[1] - pair[0]))
                    square = (y * y) * even
                    plain = even if n == 0 else plain + even
                    tilted = odd if n == 0 else tilted + odd
                    bent = square if n == 0 else bent + square
                values = (plain, x * plain, tilted, x * x * plain, x * tilted, bent)
                values = [value[0:8] + value[8:16] for value in values] + tints
                for f, value in enumerate(values):
                    for k in range(2):
                        at = slice(BLK * k, BLK * (k + 1))
                        sums[f, pl.ds(2 * j + k, 1)] = value[:, at].reshape(1, 8, BLK)
                out.append(jnp.concatenate(lasts, axis=0))
            return tuple(out)

        lax.fori_loop(0, pairs, backward, (still,) * 4)
        for h, (rows, _, _, _, _, _, sums) in enumerate(lanes):
            t = chosen[h]
            u, v, a, b, d = local(t, rows)
            m0, mx, my, mxx, mxy, myy, red, green, blue = [
                sum(sums[f, :, s, :] for s in range(8)) for f in range(FEATS)
            ]
            cx, cy = (mx - u * m0, my - v * m0)
            rows[0] = a * cx + b * cy
            rows[1] = b * cx + d * cy
            rows[2] = -0.5 * (mxx - u * (mx + cx))
            rows[3] = -(mxy - u * my - v * cx)
            rows[4] = -0.5 * (myy - v * (my + cy))
            for f, value in ((5, m0), (6, red), (7, green), (8, blue)):
                rows[f] = value

            for i in range(slots):
                slot = table_ref[0, t * slots + i]
                holder, place = slot // CAP, slot % CAP
                for f in range(FEATS):
                    back_ref[holder, f, pl.ds(place, 1), :] = rows[f, i : i + 1, :]
        return 0

    lax.fori_loop(0, tiles // 4, tile_pair, 0)


def render(table, count, arrived, goal):
    tiles = goal.shape[1]
    slots = table.shape[1] // tiles
    groups = arrived.shape[0]
    f32 = jnp.float32
    shape = jax.ShapeDtypeStruct
    return pl.pallas_call(
        render_kernel,
        out_shape=[shape((3, tiles, PIX), f32), shape((groups, FEATS, CAP, BLK), f32)],
        in_specs=[SMEM, SMEM, VMEM, VMEM],
        out_specs=[VMEM, VMEM],
        scratch_shapes=[
            pltpu.SMEM((tiles,), jnp.int32),
            pltpu.VMEM((4 * BLK, 2 * BLK), jnp.bfloat16),
            pltpu.VMEM((4 * BLK, 2 * BLK), jnp.bfloat16),
            pltpu.VMEM((PIX, 48), jnp.bfloat16),
        ]
        + [
            pltpu.VMEM(dims, f32)
            for dims in (
                (FEATS, slots, BLK),
                (48, slots, BLK),
                (slots // 2, PIX, 2 * BLK),
                (slots // 2, PIX, 2 * BLK),
                (3, PIX, BLK),
                (3, PIX, BLK),
                (FEATS, slots, 8, BLK),
            )
            for _ in range(4)
        ],
        compiler_params=params_of(40),
        name="render",
    )(table, count, arrived, goal)


def land_kernel(asked_ref, pose_ref, landed_ref, feats_ref, out_ref, total):
    total[...] = jnp.zeros_like(total)
    groups = HALF * out_ref.shape[0]

    def one(h, _):
        for c in range(CAP):
            block = asked_ref[h, 0, c]
            block = jnp.where(block < 0, 8 * groups, block)
            total[block, 0:FEATS, :] = total[block, 0:FEATS, :] + landed_ref[h, :, c, :]
        return 0

    lax.fori_loop(0, landed_ref.shape[0], one, 0, unroll=8)
    place = lax.broadcasted_iota(jnp.int32, (8, BLK), 0)
    shown = jnp.zeros((8, BLK), jnp.float32)
    for k, value in enumerate(camera_of(pose_ref)):
        shown = jnp.where(place == k, value, shown)
    for g in range(groups):
        for f in range(FEATS):
            value = total[8 * g : 8 * g + 8, f, :]
            if f >= 6:
                value = value * feats_ref[8 * g : 8 * g + 8, f + 3, :]
            out_ref[g // HALF, FEATS * (g % HALF) + f] = value
    for n in range(out_ref.shape[0]):
        out_ref[n, FEATS * HALF] = shown


def adam(weights_in, moment_one, moment_two, gradient):
    new_first = beta_one * moment_one + (1.0 - beta_one) * gradient
    new_second = beta_two * moment_two + (1.0 - beta_two) * gradient * gradient
    step_size = learn_rate / (1.0 - beta_one**ADAM_STEP)
    root = new_second * lax.rsqrt(new_second) * (1.0 / math.sqrt(1.0 - beta_two**ADAM_STEP))
    below = root + adam_eps
    inverse = pl.reciprocal(below, approx=True)
    inverse = inverse * (2.0 - below * inverse)
    return (weights_in - step_size * new_first * inverse, new_first, new_second)


def update_kernel(
    params_ref, first_ref, second_ref, own_ref, next_ref, low_ref, high_ref, last_ref,
    new_params_ref, new_first_ref, new_second_ref, pulls, turned, shades, waves, ready, sent,
):
    me = lax.axis_index("view")
    views = 4
    outs = (new_params_ref, new_first_ref, new_second_ref)
    steps = HALF * own_ref.shape[0]
    chunk = 8 * BLK
    for k, ref in ((0, own_ref), (1, next_ref), (3, last_ref)):
        pulls[(me + k) % views] = ref[...]
    for k, ref in enumerate((low_ref, high_ref)):
        pulls[(me + 2) % views, k] = ref[0]
    cameras = [[pulls[v, 0, FEATS * HALF, k : k + 1, :] for k in range(6)] for v in range(views)]
    for v in range(views):
        terms = look_terms(cameras[v])
        for k in range(8):
            row = lax.broadcasted_iota(jnp.int32, (8, BLK), 0) + (8 * k - 11)
            wave = jnp.zeros((8, BLK), jnp.float32)
            for j in range(16):
                wave = jnp.where((row >= 0) & (row % 16 == j), terms[j], wave)
            waves[v, 8 * k : 8 * k + 8, :] = wave

    def plus(left, right):
        return right if left is None else [p + q for p, q in zip(left, right)]

    def copies(step):
        slot = step % 2
        at = slice(step * chunk, (step + 1) * chunk)
        return [
            pltpu.make_async_copy(ready.at[slot, n], outs[n].at[:, at], sent.at[slot, n])
            for n in range(3)
        ]

    row_in = lax.broadcasted_iota(jnp.int32, (8, BLK), 0)
    for step in range(steps):
        base = step * chunk
        for j in range(8):
            turned[j] = params_ref[0:16, base + j * BLK : base + (j + 1) * BLK]

        rows = [turned[:, r, :] for r in range(11)]
        opacity = 1.0 / (1.0 + jnp.exp(-rows[10]))
        matrix, pull_frame = jax.vjp(frame, *rows[3:10])
        centre, bent = (None, None)
        for v in range(views):
            right, upward = axes(cameras[v])
            seen = [pulls[v, step // HALF, FEATS * (step % HALF) + f] for f in range(FEATS)]
            across, downward = (16.0 * seen[0], 16.0 * seen[1])
            moved = [
                right[0] * across + upward[0] * downward,
                upward[1] * downward,
                right[1] * across + upward[2] * downward,
                seen[5],
            ]
            centre = plus(centre, moved)
            bent = plus(bent, conic_pull(matrix, cameras[v], seen[2:5]))
            for c in range(3):
                shades[:, 3 * v + c, :] = seen[6 + c]
        total = centre[0:3] + list(pull_frame(tuple(bent))) + [centre[3] * (1.0 - opacity)]
        for r in range(11):
            turned[:, r, :] = total[r]
        if step >= 2:
            for copy in copies(step - 2):
                copy.wait()
        slot = step % 2
        for j in range(8):
            columns = slice(base + j * BLK, base + (j + 1) * BLK)
            for k in range(8):
                gradient = None
                if k > 0:
                    first = (8 * k - 11) // 16 if k > 1 else 0
                    last = min((8 * k + 7 - 11) // 16, 2)
                    for v in range(views):
                        tint = shades[j, 3 * v + first : 3 * v + first + 1, :]
                        if last != first:
                            tint = jnp.where(
                                row_in + (8 * k - 11) < 16 * last,
                                tint,
                                shades[j, 3 * v + last : 3 * v + last + 1, :],
                            )
                        term = waves[v, 8 * k : 8 * k + 8, :] * tint
                        gradient = term if gradient is None else gradient + term
                if k == 0:
                    gradient = turned[j, 0:8, :]
                if k == 1:
                    gradient = jnp.where(row_in < 3, turned[j, 8:16, :], gradient)
                height = min(8, PARAMS - 8 * k)
                at = (slice(8 * k, 8 * k + height), columns)
                values = adam(params_ref[at], first_ref[at], second_ref[at], gradient[0:height])
                for n in range(3):
                    ready[slot, n, 8 * k : 8 * k + height, j * BLK : (j + 1) * BLK] = values[n]
        for copy in copies(step):
            copy.start()
    for step in range(max(steps - 2, 0), steps):
        for copy in copies(step):
            copy.wait()


def project(view_pose, gauss_params):
    columns = gauss_params.shape[1]
    blocks = columns // BLK
    f32 = jnp.float32
    shape = jax.ShapeDtypeStruct
    chunk = PROJECT_BLOCKS * BLK
    wide = pl.BlockSpec((PARAMS, chunk), lambda i: (0, i))
    steps = columns // chunk
    return pl.pallas_call(
        project_kernel,
        grid=(steps,),
        out_shape=shape((blocks, 16, BLK), f32),
        in_specs=[SMEM, wide],
        out_specs=pl.BlockSpec((PROJECT_BLOCKS, 16, BLK), lambda i: (i, 0, 0)),
        scratch_shapes=[
            pltpu.VMEM((PROJECT_BLOCKS, 16, BLK), f32),
            pltpu.VMEM((8, BLK), f32),
            pltpu.VMEM((3, 24, BLK), f32),
        ],
        compiler_params=params_of(PROJECT_MB),
        name="project",
    )(view_pose, gauss_params)


def update(gauss_params, first_moment, second_moment, own, after, low, high, prior):
    f32 = jnp.float32
    views = 4
    chunk = 8 * BLK
    return pl.pallas_call(
        update_kernel,
        out_shape=[jax.ShapeDtypeStruct(gauss_params.shape, f32)] * 3,
        in_specs=[VMEM] * 8,
        out_specs=[pl.BlockSpec(memory_space=pl.ANY)] * 3,
        scratch_shapes=[
            pltpu.VMEM((views, *own.shape), f32),
            pltpu.VMEM((8, 16, BLK), f32),
            pltpu.VMEM((8, 16, BLK), f32),
            pltpu.VMEM((views, 64, BLK), f32),
            pltpu.VMEM((2, 3, PARAMS, chunk), f32),
            pltpu.SemaphoreType.DMA((2, 3)),
        ],
        compiler_params=params_of(UPDATE_MB),
        name="update",
    )(gauss_params, first_moment, second_moment, own, after, low, high, prior)


def shards(
    gauss_params, first_moment, second_moment, view_pose, tile_blocks, tile_order, target_image
):
    groups = lax.axis_size("gs")
    views = lax.axis_size("view")
    columns = gauss_params.shape[1]
    blocks = columns // BLK
    tiles, slots = tile_blocks.shape[1:]
    f32, i32 = jnp.float32, jnp.int32
    shape = jax.ShapeDtypeStruct

    wanted, table, count = pl.pallas_call(
        request_kernel,
        out_shape=[shape((groups, 1, CAP), i32)] + [shape((1, tiles * slots), i32)] * 2,
        in_specs=[VMEM, VMEM],
        out_specs=[VMEM, VMEM, VMEM],
        name="requests",
    )(tile_blocks[0], tile_order[0])
    asked = lax.all_to_all(wanted, "gs", split_axis=0, concat_axis=0, tiled=True)
    feats = project(view_pose, gauss_params)
    outgoing = pl.pallas_call(
        pick_kernel,
        out_shape=shape((groups, FEATS, CAP, BLK), f32),
        in_specs=[SMEM, VMEM],
        out_specs=VMEM,
        compiler_params=params_of(16),
        name="pick",
    )(asked, feats)
    arrived = lax.all_to_all(outgoing, "gs", split_axis=0, concat_axis=0, tiled=True)
    image, back = render(table, count, arrived, jnp.transpose(target_image[0], (1, 0, 2)))
    landed = lax.all_to_all(back, "gs", split_axis=0, concat_axis=0, tiled=True)
    own = pl.pallas_call(
        land_kernel,
        out_shape=shape((blocks // (8 * HALF), FEATS * HALF + 1, 8, BLK), f32),
        in_specs=[SMEM, SMEM, VMEM, VMEM],
        out_specs=VMEM,
        scratch_shapes=[pltpu.VMEM((blocks + 1, 16, BLK), f32)],
        compiler_params=params_of(16),
        name="land",
    )(asked, view_pose, landed, feats)

    def from_next(value, k):
        return lax.ppermute(value, "view", [((i + k) % views, i) for i in range(views)])

    after = from_next(own, 1)
    prior = from_next(own, views - 1)
    low = from_next(after[:1], 1)
    high = from_next(prior[1:], views - 1)
    new_params, new_first, new_second = update(
        gauss_params, first_moment, second_moment, own, after, low, high, prior
    )
    return (new_params, new_first, new_second, jnp.transpose(image, (1, 0, 2))[None])


def solution(mesh):
    placed = (
        P(None, "gs"),
        P(None, "gs"),
        P(None, "gs"),
        P("view", None),
        P("view", "gs", None),
        P("view", "gs", None),
        P("view", "gs", None, None),
    )
    return jax.shard_map(
        shards,
        mesh=mesh,
        in_specs=placed,
        out_specs=(P(None, "gs"), P(None, "gs"), P(None, "gs"), P("view", "gs", None, None)),
        check_vma=False,
    )
```

```python
import functools
import math

import jax
import jax.numpy as jnp
from jax import lax
from jax.experimental import pallas as pl
from jax.experimental.pallas import tpu as pltpu
from jax.sharding import PartitionSpec as P

PARAMS = 59
BLK = 128
PIX = 256
FEATS = 9
CAP = 2
ADAM_STEP = 20

beta_one = 0.9
beta_two = 0.999
learn_rate = 0.01
adam_eps = 1e-08
dilation = 0.3
LOG2E = 1.4426950408889634
TINY = 1.1754944e-38
BELOW_ONE = 0.99999994
PROJECT_MB = 24
UPDATE_MB = 24
PROJECT_BLOCKS = 32
ROWS = 64
HALF = 4

VMEM = pl.BlockSpec(memory_space=pltpu.VMEM)
SMEM = pl.BlockSpec(memory_space=pltpu.SMEM)


def params_of(megabytes):
    return pltpu.CompilerParams(vmem_limit_bytes=megabytes << 20)


def harmonics(x, y, z):
    square_x, square_y, square_z = (x * x, y * y, z * z)
    return [
        0.28209479177387814 + 0.0 * x,
        -0.4886025119029199 * y,
        0.4886025119029199 * z,
        -0.4886025119029199 * x,
        1.0925484305920792 * x * y,
        -1.0925484305920792 * y * z,
        0.31539156525252005 * (2.0 * square_z - square_x - square_y),
        -1.0925484305920792 * x * z,
        0.5462742152960396 * (square_x - square_y),
        -0.5900435899266435 * y * (3.0 * square_x - square_y),
        2.890611442640554 * x * y * z,
        -0.4570457994644658 * y * (4.0 * square_z - square_x - square_y),
        0.3731763325901154 * z * (2.0 * square_z - 3.0 * square_x - 3.0 * square_y),
        -0.4570457994644658 * x * (4.0 * square_z - square_x - square_y),
        1.445305721320277 * z * (square_x - square_y),
        -0.5900435899266435 * x * (square_x - 3.0 * square_y),
    ]


def camera_of(pose_ref):
    yaw, tilt, shift_x, shift_y = [jnp.full((1, BLK), pose_ref[0, k]) for k in range(4)]
    return [jnp.sin(yaw), jnp.cos(yaw), jnp.sin(tilt), jnp.cos(tilt), shift_x, shift_y]


def look_terms(camera):
    sin_yaw, cos_yaw, sin_tilt, cos_tilt = camera[0:4]
    return harmonics(sin_yaw * cos_tilt, -sin_tilt, cos_yaw * cos_tilt)


def axes(camera):
    sin_yaw, cos_yaw, sin_tilt, cos_tilt = camera[0:4]
    return (cos_yaw, -sin_yaw), (sin_yaw * sin_tilt, cos_tilt, cos_yaw * sin_tilt)


def frame(*rows):
    scales = [16.0 * jnp.exp(value) for value in rows[0:3]]
    w, x, y, z = rows[3:7]
    inverse = lax.rsqrt(jnp.maximum(w * w + x * x + y * y + z * z, 1.0))
    w, x, y, z = (w * inverse, x * inverse, y * inverse, z * inverse)
    rotation = (
        (1.0 - 2.0 * (y * y + z * z), 2.0 * (x * y - w * z), 2.0 * (x * z + w * y)),
        (2.0 * (x * y + w * z), 1.0 - 2.0 * (x * x + z * z), 2.0 * (y * z - w * x)),
        (2.0 * (x * z - w * y), 2.0 * (y * z + w * x), 1.0 - 2.0 * (x * x + y * y)),
    )
    return tuple(scales[k] * rotation[r][k] for r in range(3) for k in range(3))


def spreads(matrix, camera):
    right, upward = axes(camera)
    first = [right[0] * matrix[k] + right[1] * matrix[6 + k] for k in range(3)]
    second = [
        upward[0] * matrix[k] + upward[1] * matrix[3 + k] + upward[2] * matrix[6 + k]
        for k in range(3)
    ]
    spread_first = first[0] * first[0] + first[1] * first[1] + first[2] * first[2] + dilation
    spread_mixed = first[0] * second[0] + first[1] * second[1] + first[2] * second[2]
    spread_second = second[0] * second[0] + second[1] * second[1] + second[2] * second[2] + dilation
    determinant = spread_first * spread_second - spread_mixed * spread_mixed
    return first, second, spread_first, spread_mixed, spread_second, determinant


def conic(matrix, camera):
    _, _, spread_first, spread_mixed, spread_second, determinant = spreads(matrix, camera)
    return (spread_second / determinant, -spread_mixed / determinant, spread_first / determinant)


def conic_pull(matrix, camera, pulls):
    right, upward = axes(camera)
    first, second, spread_first, spread_mixed, spread_second, determinant = spreads(matrix, camera)
    inverse = 1.0 / determinant
    pull_a, pull_b, pull_c = [value * inverse for value in pulls]
    shrink = (pull_b * spread_mixed - pull_a * spread_second - pull_c * spread_first) * inverse
    to_first = 2.0 * (pull_c + shrink * spread_second)
    to_second = 2.0 * (pull_a + shrink * spread_first)
    to_mixed = -pull_b - 2.0 * (shrink * spread_mixed)
    on_first = [to_first * p + to_mixed * q for p, q in zip(first, second)]
    on_second = [to_second * q + to_mixed * p for p, q in zip(first, second)]
    return (
        [right[0] * p + upward[0] * q for p, q in zip(on_first, on_second)]
        + [upward[1] * q for q in on_second]
        + [right[1] * p + upward[2] * q for p, q in zip(on_first, on_second)]
    )


def geometry(rows, camera):
    right, upward = axes(camera)
    across = 16.0 * (right[0] * rows[0] + right[1] * rows[2]) + camera[4]
    downward = 16.0 * (upward[0] * rows[0] + upward[1] * rows[1] + upward[2] * rows[2]) + camera[5]
    return [across, downward, *conic(frame(*rows[3:10]), camera)]


def split(value, parts):
    out = []
    for _ in range(parts - 1):
        high = value.astype(jnp.bfloat16).astype(jnp.float32)
        out.append(high)
        value = value - high
    out.append(value)
    return out


def request_kernel(blocks_ref, order_ref, wanted_ref, table_ref, count_ref):
    tiles, slots = blocks_ref.shape
    holders = wanted_ref.shape[0]
    count = tiles * slots
    by_holder = 6
    by_tile = 4

    def flat(ref):
        return jnp.concatenate([ref[t : t + 1, :] for t in range(tiles)], axis=1)

    def spread(row):
        return jnp.broadcast_to(row, (count, count))

    def add(keep, value, axis):
        return jnp.sum(jnp.where(keep, value, 0.0), axis=axis, keepdims=True)

    def whole(value):
        return value.astype(jnp.int32)

    row = lax.broadcasted_iota(jnp.int32, (count, count), 0)
    lane = lax.broadcasted_iota(jnp.int32, (count, count), 1)
    row_tile, lane_tile = (row >> by_tile, lane >> by_tile)
    block = spread(flat(blocks_ref))
    holder = block >> by_holder
    earlier = whole(add((holder.T == holder) & (row < lane), 1.0, 0))
    slot = spread(jnp.where(block[0:1] >= 0, holder[0:1] * CAP + earlier, -1))
    within = (block - (holder << by_holder) + 1).astype(jnp.float32)
    wanted = [
        whole(add(slot[0:holders] == CAP * row[0:holders] + c, within[0:holders], 1)) - 1
        for c in range(CAP)
    ]
    wanted = jnp.where(lane[0:holders] == 0, wanted[0], wanted[1])
    for h in range(holders):
        wanted_ref[h] = wanted[h : h + 1, 0:CAP]
    filled = add(slot.T == lane, 1.0, 0)
    spare = jnp.max(
        jnp.where(filled > 0.0, 0.0, lane[0:1].astype(jnp.float32)), axis=1, keepdims=True
    )
    place = spread(flat(order_ref) + (lane_tile[0:1] << by_tile)).T
    chosen = add(place == lane, (slot + 1).astype(jnp.float32), 1) - 1.0
    used = jnp.broadcast_to((chosen >= 0.0).astype(jnp.float32), (count, count))
    same = row_tile == lane_tile
    rank = whole(add(same & (lane < row), used.T, 1))
    target = jnp.where(chosen >= 0.0, (row[:, 0:1] & -slots) + rank, -1)
    table_ref[...] = whole(add(target == lane, chosen - spare, 0) + spare)
    count_ref[...] = whole(add(row_tile == lane, used, 0))


def project_kernel(pose_ref, params_ref, feats_ref, turned, seen, weight):
    @pl.when(pl.program_id(0) == 0)
    def _():
        camera = camera_of(pose_ref)
        for k in range(6):
            seen[k : k + 1, :] = camera[k]
        terms = look_terms(camera)
        for c in range(3):
            row = lax.broadcasted_iota(jnp.int32, (24, BLK), 0) - 3
            value = jnp.zeros((24, BLK), jnp.float32)
            for j in range(16):
                value = jnp.where(row == j, terms[j], value)
            weight[c] = value

    camera = [seen[k : k + 1, :] for k in range(6)]
    for j in range(PROJECT_BLOCKS):
        turned[j] = params_ref[0:16, j * BLK : (j + 1) * BLK]
    for j in range(PROJECT_BLOCKS):
        columns = slice(j * BLK, (j + 1) * BLK)
        for c in range(3):
            low = 16 * c + 8
            high = min(low + 24, PARAMS)
            terms = params_ref[low : low + 16, columns] * weight[c, 0:16]
            ends = params_ref[low + 16 : high, columns] * weight[c, 16 : high - low]
            terms = terms[0:8] + terms[8:16]
            if high - low == 24:
                shade = jnp.sum(terms + ends, axis=0, keepdims=True)
            else:
                shade = jnp.sum(terms, axis=0, keepdims=True) + jnp.sum(ends, axis=0, keepdims=True)
            shade = 0.5 + shade
            mask = jnp.where(shade > 0.0, 1.0, jnp.where(shade == 0.0, 0.5, 0.0))
            feats_ref[j, 6 + c : 7 + c, :] = jnp.maximum(shade, 0.0)
            feats_ref[j, 9 + c : 10 + c, :] = mask
    rows = [turned[:, r, :] for r in range(11)]
    opacity = 1.0 / (1.0 + jnp.exp(-rows[10]))
    for r, value in enumerate(geometry(rows, camera) + [opacity]):
        feats_ref[:, r, :] = value


def pick_kernel(asked_ref, feats_ref, out_ref):
    def one(h, _):
        for c in range(CAP):
            block = lax.max(asked_ref[h, 0, c], 0)
            out_ref[h, :, c, :] = feats_ref[block][0:FEATS]
        return 0

    lax.fori_loop(0, out_ref.shape[0], one, 0, unroll=8)


def bands(earlier):
    row = lax.broadcasted_iota(jnp.int32, (4 * BLK, 2 * BLK), 0) % (2 * BLK)
    column = lax.broadcasted_iota(jnp.int32, (4 * BLK, 2 * BLK), 1)
    inside = row < column if earlier else row > column
    return inside.astype(jnp.float32).astype(jnp.bfloat16)


def halves_of(value):
    high = value.astype(jnp.bfloat16)
    low = (value - high.astype(jnp.float32)).astype(jnp.bfloat16)
    return jnp.concatenate([high, low], axis=1)


def across(value, wide):
    return jnp.concatenate([value] * wide, axis=1)


def band_of(band, wide):
    size = wide * BLK
    return jnp.concatenate([band[0:size, 0:size], band[2 * BLK : 2 * BLK + size, 0:size]], axis=0)


def render_kernel(
    table_ref,
    count_ref,
    arrived_ref,
    goal_ref,
    image_ref,
    back_ref,
    ranked,
    before,
    after,
    basis,
    *buffers,
):
    my_row = lax.axis_index("gs")
    lanes = tuple(buffers[h::4] for h in range(4))
    tiles = goal_ref.shape[1]
    slots = table_ref.shape[1] // tiles
    before[...] = bands(True)
    after[...] = bands(False)
    pixel = lax.broadcasted_iota(jnp.int32, (PIX, 48), 0)
    place = lax.broadcasted_iota(jnp.int32, (PIX, 48), 1)
    x = (pixel % 16).astype(jnp.float32) - 7.5
    y = (pixel // 16).astype(jnp.float32) - 7.5
    powers = jnp.where((place < 24) & (place % 8 == 0), 1.0, 0.0)
    for k, value in enumerate((x, y, x * x, x * y, y * y)):
        powers = jnp.where((place < 24) & (place % 8 == k + 1), value, powers)
    basis[...] = powers.astype(jnp.bfloat16)
    x = lax.broadcasted_iota(jnp.int32, (16, 2 * BLK), 0).astype(jnp.float32) - 7.5
    blank = jnp.zeros((8, PIX), jnp.float32)
    slot_at = lax.broadcasted_iota(jnp.int32, (slots, BLK), 0)
    for _, terms, *_ in lanes:
        terms[...] = jnp.zeros_like(terms)
    counts = [count_ref[0, t] for t in range(tiles)]
    for t in range(tiles):
        rank = jnp.int32(0)
        for s in range(tiles):
            ahead = counts[s] >= counts[t] if s < t else counts[s] > counts[t]
            if s != t:
                rank = rank + ahead.astype(jnp.int32)
        ranked[rank] = t

    def side_by_side(ref, at, j, wide):
        return jnp.concatenate(
            [ref[at, pl.ds(2 * j + k, 1), :].reshape(-1, BLK) for k in range(wide)], axis=1
        )

    def local(t, rows):
        u = rows[0] - (16 * t + 8).astype(jnp.float32)
        v = rows[1] - (16 * my_row + 8).astype(jnp.float32)
        return u, v, rows[2], rows[3], rows[4]

    def prepare(t, used, rows, terms):
        for i in range(slots):
            slot = table_ref[0, t * slots + i]
            holder, place = slot // CAP, slot % CAP
            for f in range(FEATS):
                rows[f, i : i + 1, :] = arrived_ref[holder, f, pl.ds(place, 1), :]
        u, v, a, b, d = local(t, rows)
        au, bv = (a * u + b * v, b * u + d * v)
        full = jnp.log2(jnp.maximum(rows[5], TINY)) - (0.5 * LOG2E) * (au * u + bv * v)
        shape = [full, LOG2E * au, LOG2E * bv, (-0.5 * LOG2E) * a, -LOG2E * b, (-0.5 * LOG2E) * d]
        for k, value in enumerate(shape):
            value = jnp.where(slot_at < used, value, -2e4 if k == 0 else 0.0)
            for p, part in enumerate(split(value, 3)):
                terms[8 * p + k] = part
        for k in range(3):
            tint = jnp.where(slot_at < used, rows[6 + k], 0.0)
            rows[6 + k] = tint
            high, mid, low = split(tint, 3)
            for p, part in enumerate((high, high, mid, high, low, mid)):
                terms[24 + 3 * p + k] = part

    def tile_pair(g, _):
        chosen = [ranked[4 * g + h] for h in range(4)]
        used = [count_ref[0, t] for t in chosen]
        most = functools.reduce(lax.max, used)
        pairs, odd_one = (most // 2, most % 2)
        for h, (rows, terms, _, _, shades, _, _) in enumerate(lanes):
            prepare(chosen[h], used[h], rows, terms)
            shades[...] = jnp.zeros_like(shades)

        def forward(j, logs, wide):
            size = wide * BLK
            state = []
            for rows, terms, *_ in lanes:
                coefs = side_by_side(terms, slice(None), j, wide).astype(jnp.bfloat16)
                state.append(jnp.dot(basis[...], coefs, preferred_element_type=jnp.float32))
            alphas, losses, halves = ([], [], [])
            for h, (_, _, ratios, *_) in enumerate(lanes):
                for r in range(0, PIX, ROWS):
                    alpha = jnp.minimum(jnp.exp2(state[h][r : r + ROWS]), BELOW_ONE)
                    loss = jnp.log2(1.0 - alpha)
                    ratios[j, r : r + ROWS, 0:size] = alpha * jnp.exp2(-loss)
                    alphas.append(alpha)
                    losses.append(loss)
                    halves.append(halves_of(loss))
            run = jnp.dot(
                jnp.concatenate(halves, axis=0), band_of(before, wide), preferred_element_type=jnp.float32
            )
            out = []
            for h, (rows, _, _, weights, shades, _, _) in enumerate(lanes):
                tints = side_by_side(rows, slice(6, 9), j, wide)
                lasts = []
                for r in range(0, PIX, ROWS):
                    n = (h * PIX + r) // ROWS
                    mine = run[h * PIX + r : h * PIX + r + ROWS]
                    log = logs[h][r : r + ROWS]
                    weight = alphas[n] * jnp.exp2(mine + across(log, wide))
                    weights[j, r : r + ROWS, 0:size] = weight
                    for c in range(3):
                        shade = weight * tints[c : c + 1]
                        if wide == 2:
                            shade = shade[:, 0:BLK] + shade[:, BLK:]
                        shades[c, r : r + ROWS] += shade
                    last = mine[:, size - 1 :] + losses[n][:, size - 1 :]
                    lasts.append(log + jnp.broadcast_to(last, (ROWS, BLK)))
                out.append(jnp.concatenate(lasts, axis=0))
            return tuple(out)

        still = jnp.zeros((PIX, BLK), jnp.float32)
        logs = lax.fori_loop(0, pairs, functools.partial(forward, wide=2), (still,) * 4)

        @pl.when(odd_one == 1)
        def _():
            forward(pairs, logs, 1)

        lane = lax.broadcasted_iota(jnp.int32, (PIX, BLK), 1)
        pulled = []
        for h, (_, _, _, _, shades, pulls, _) in enumerate(lanes):
            columns = jnp.zeros((PIX, BLK), jnp.float32)
            for c in range(3):
                columns = jnp.where(lane == c, jnp.sum(shades[c], axis=1, keepdims=True), columns)
            image = columns.T[0:3]
            at = pl.ds(chosen[h], 1)
            for c in range(3):
                image_ref[c, at, :] = image[c : c + 1]
            pull = image - jnp.concatenate([goal_ref[c, at, :] for c in range(3)], axis=0)
            high, mid, low = split(pull, 3)
            turned = jnp.concatenate(
                [blank] * 3 + [high, mid, high, low, high, mid, pull, blank[0:3]], axis=0
            ).T
            for c in range(3):
                pulls[c] = jnp.broadcast_to(turned[:, 42 + c : 43 + c], (PIX, BLK))
            pulled.append(turned.astype(jnp.bfloat16))

        def backward(step, later, wide):
            j = pairs - 1 - step
            size = wide * BLK
            tilt = x[:, 0:size]
            reaches, halves = ([], [])
            for h, (_, terms, _, weights, *_) in enumerate(lanes):
                coefs = side_by_side(terms, slice(None), j, wide).astype(jnp.bfloat16)
                pull = jnp.dot(pulled[h], coefs, preferred_element_type=jnp.float32)
                for r in range(0, PIX, 16):
                    reach = pull[r : r + 16] * weights[j, r : r + 16, 0:size]
                    reaches.append(reach)
                    halves.append(halves_of(reach))
            behinds = jnp.dot(
                jnp.concatenate(halves, axis=0), band_of(after, wide), preferred_element_type=jnp.float32
            )
            out = []
            for h, (_, _, ratios, weights, _, pulls, sums) in enumerate(lanes):
                plain, tilted, bent = (None, None, None)
                tints = [None] * 3
                lasts = [None] * 16
                for n in range(8):
                    pair = []
                    for m in (n, 15 - n):
                        at = slice(16 * m, 16 * m + 16)
                        reach = reaches[16 * h + m]
                        behind = behinds[h * PIX + 16 * m : h * PIX + 16 * m + 16]
                        log = later[h][at]
                        pair.append(reach - (behind + across(log, wide)) * ratios[j, at, 0:size])
                        last = jnp.broadcast_to(behind[:, 0:1] + reach[:, 0:1], (16, BLK))
                        lasts[m] = log + last
                        weight = weights[j, at, 0:size]
                        for c in range(3):
                            tint = weight * across(pulls[c, at], wide)
                            tint = tint[0:8] + tint[8:16]
                            tints[c] = tint if tints[c] is None else tints[c] + tint
                    y = 7.5 - n
                    even, odd = (pair[1] + pair[0], y * (pair[1] - pair[0]))
                    square = (y * y) * even
                    plain = even if n == 0 else plain + even
                    tilted = odd if n == 0 else tilted + odd
                    bent = square if n == 0 else bent + square
                values = (plain, tilt * plain, tilted, tilt * tilt * plain, tilt * tilted, bent)
                values = [value[0:8] + value[8:16] for value in values] + tints
                for f, value in enumerate(values):
                    for k in range(wide):
                        at = slice(BLK * k, BLK * (k + 1))
                        sums[f, pl.ds(2 * j + k, 1)] = value[:, at].reshape(1, 8, BLK)
                out.append(jnp.concatenate(lasts, axis=0))
            return tuple(out)

        later = lax.fori_loop(
            0, odd_one, lambda _, later: backward(-1, later, 1), (still,) * 4
        )
        lax.fori_loop(0, pairs, functools.partial(backward, wide=2), later)
        for h, (rows, _, _, _, _, _, sums) in enumerate(lanes):
            t = chosen[h]
            u, v, a, b, d = local(t, rows)
            m0, mx, my, mxx, mxy, myy, red, green, blue = [
                sum(sums[f, :, s, :] for s in range(8)) for f in range(FEATS)
            ]
            cx, cy = (mx - u * m0, my - v * m0)
            rows[0] = a * cx + b * cy
            rows[1] = b * cx + d * cy
            rows[2] = -0.5 * (mxx - u * (mx + cx))
            rows[3] = -(mxy - u * my - v * cx)
            rows[4] = -0.5 * (myy - v * (my + cy))
            for f, value in ((5, m0), (6, red), (7, green), (8, blue)):
                rows[f] = value

            for i in range(slots):
                slot = table_ref[0, t * slots + i]
                holder, place = slot // CAP, slot % CAP
                for f in range(FEATS):
                    back_ref[holder, f, pl.ds(place, 1), :] = rows[f, i : i + 1, :]
        return 0

    lax.fori_loop(0, tiles // 4, tile_pair, 0)


def render(table, count, arrived, goal):
    tiles = goal.shape[1]
    slots = table.shape[1] // tiles
    groups = arrived.shape[0]
    f32 = jnp.float32
    shape = jax.ShapeDtypeStruct
    return pl.pallas_call(
        render_kernel,
        out_shape=[shape((3, tiles, PIX), f32), shape((groups, FEATS, CAP, BLK), f32)],
        in_specs=[SMEM, SMEM, VMEM, VMEM],
        out_specs=[VMEM, VMEM],
        scratch_shapes=[
            pltpu.SMEM((tiles,), jnp.int32),
            pltpu.VMEM((4 * BLK, 2 * BLK), jnp.bfloat16),
            pltpu.VMEM((4 * BLK, 2 * BLK), jnp.bfloat16),
            pltpu.VMEM((PIX, 48), jnp.bfloat16),
        ]
        + [
            pltpu.VMEM(dims, f32)
            for dims in (
                (FEATS, slots, BLK),
                (48, slots, BLK),
                (slots // 2, PIX, 2 * BLK),
                (slots // 2, PIX, 2 * BLK),
                (3, PIX, BLK),
                (3, PIX, BLK),
                (FEATS, slots, 8, BLK),
            )
            for _ in range(4)
        ],
        compiler_params=params_of(40),
        name="render",
    )(table, count, arrived, goal)


def land_kernel(asked_ref, pose_ref, landed_ref, feats_ref, out_ref, total):
    total[...] = jnp.zeros_like(total)
    groups = HALF * out_ref.shape[0]

    def one(h, _):
        for c in range(CAP):
            block = asked_ref[h, 0, c]
            block = jnp.where(block < 0, 8 * groups, block)
            total[block, 0:FEATS, :] = total[block, 0:FEATS, :] + landed_ref[h, :, c, :]
        return 0

    lax.fori_loop(0, landed_ref.shape[0], one, 0, unroll=8)
    place = lax.broadcasted_iota(jnp.int32, (8, BLK), 0)
    shown = jnp.zeros((8, BLK), jnp.float32)
    for k, value in enumerate(camera_of(pose_ref)):
        shown = jnp.where(place == k, value, shown)
    for g in range(groups):
        for f in range(FEATS):
            value = total[8 * g : 8 * g + 8, f, :]
            if f >= 6:
                value = value * feats_ref[8 * g : 8 * g + 8, f + 3, :]
            out_ref[g // HALF, FEATS * (g % HALF) + f] = value
    for n in range(out_ref.shape[0]):
        out_ref[n, FEATS * HALF] = shown


def adam(weights_in, moment_one, moment_two, gradient):
    new_first = beta_one * moment_one + (1.0 - beta_one) * gradient
    new_second = beta_two * moment_two + (1.0 - beta_two) * gradient * gradient
    step_size = learn_rate / (1.0 - beta_one**ADAM_STEP)
    root = new_second * lax.rsqrt(new_second) * (1.0 / math.sqrt(1.0 - beta_two**ADAM_STEP))
    below = root + adam_eps
    inverse = pl.reciprocal(below, approx=True)
    inverse = inverse * (2.0 - below * inverse)
    return (weights_in - step_size * new_first * inverse, new_first, new_second)


def update_kernel(
    params_ref, first_ref, second_ref, own_ref, next_ref, low_ref, high_ref, last_ref,
    new_params_ref, new_first_ref, new_second_ref, pulls, turned, shades, waves, ready, sent,
):
    me = lax.axis_index("view")
    views = 4
    outs = (new_params_ref, new_first_ref, new_second_ref)
    steps = HALF * own_ref.shape[0]
    chunk = 8 * BLK
    for k, ref in ((0, own_ref), (1, next_ref), (3, last_ref)):
        pulls[(me + k) % views] = ref[...]
    for k, ref in enumerate((low_ref, high_ref)):
        pulls[(me + 2) % views, k] = ref[0]
    cameras = [[pulls[v, 0, FEATS * HALF, k : k + 1, :] for k in range(6)] for v in range(views)]
    for v in range(views):
        terms = look_terms(cameras[v])
        for k in range(8):
            row = lax.broadcasted_iota(jnp.int32, (8, BLK), 0) + (8 * k - 11)
            wave = jnp.zeros((8, BLK), jnp.float32)
            for j in range(16):
                wave = jnp.where((row >= 0) & (row % 16 == j), terms[j], wave)
            waves[v, 8 * k : 8 * k + 8, :] = wave

    def plus(left, right):
        return right if left is None else [p + q for p, q in zip(left, right)]

    def copies(step):
        slot = step % 2
        at = slice(step * chunk, (step + 1) * chunk)
        return [
            pltpu.make_async_copy(ready.at[slot, n], outs[n].at[:, at], sent.at[slot, n])
            for n in range(3)
        ]

    row_in = lax.broadcasted_iota(jnp.int32, (8, BLK), 0)
    for step in range(steps):
        base = step * chunk
        for j in range(8):
            turned[j] = params_ref[0:16, base + j * BLK : base + (j + 1) * BLK]

        rows = [turned[:, r, :] for r in range(11)]
        opacity = 1.0 / (1.0 + jnp.exp(-rows[10]))
        matrix, pull_frame = jax.vjp(frame, *rows[3:10])
        centre, bent = (None, None)
        for v in range(views):
            right, upward = axes(cameras[v])
            seen = [pulls[v, step // HALF, FEATS * (step % HALF) + f] for f in range(FEATS)]
            across, downward = (16.0 * seen[0], 16.0 * seen[1])
            moved = [
                right[0] * across + upward[0] * downward,
                upward[1] * downward,
                right[1] * across + upward[2] * downward,
                seen[5],
            ]
            centre = plus(centre, moved)
            bent = plus(bent, conic_pull(matrix, cameras[v], seen[2:5]))
            for c in range(3):
                shades[:, 3 * v + c, :] = seen[6 + c]
        total = centre[0:3] + list(pull_frame(tuple(bent))) + [centre[3] * (1.0 - opacity)]
        for r in range(11):
            turned[:, r, :] = total[r]
        if step >= 2:
            for copy in copies(step - 2):
                copy.wait()
        slot = step % 2
        for j in range(8):
            columns = slice(base + j * BLK, base + (j + 1) * BLK)
            for k in range(8):
                gradient = None
                if k > 0:
                    first = (8 * k - 11) // 16 if k > 1 else 0
                    last = min((8 * k + 7 - 11) // 16, 2)
                    for v in range(views):
                        tint = shades[j, 3 * v + first : 3 * v + first + 1, :]
                        if last != first:
                            tint = jnp.where(
                                row_in + (8 * k - 11) < 16 * last,
                                tint,
                                shades[j, 3 * v + last : 3 * v + last + 1, :],
                            )
                        term = waves[v, 8 * k : 8 * k + 8, :] * tint
                        gradient = term if gradient is None else gradient + term
                if k == 0:
                    gradient = turned[j, 0:8, :]
                if k == 1:
                    gradient = jnp.where(row_in < 3, turned[j, 8:16, :], gradient)
                height = min(8, PARAMS - 8 * k)
                at = (slice(8 * k, 8 * k + height), columns)
                values = adam(params_ref[at], first_ref[at], second_ref[at], gradient[0:height])
                for n in range(3):
                    ready[slot, n, 8 * k : 8 * k + height, j * BLK : (j + 1) * BLK] = values[n]
        for copy in copies(step):
            copy.start()
    for step in range(max(steps - 2, 0), steps):
        for copy in copies(step):
            copy.wait()


def project(view_pose, gauss_params):
    columns = gauss_params.shape[1]
    blocks = columns // BLK
    f32 = jnp.float32
    shape = jax.ShapeDtypeStruct
    chunk = PROJECT_BLOCKS * BLK
    wide = pl.BlockSpec((PARAMS, chunk), lambda i: (0, i))
    steps = columns // chunk
    return pl.pallas_call(
        project_kernel,
        grid=(steps,),
        out_shape=shape((blocks, 16, BLK), f32),
        in_specs=[SMEM, wide],
        out_specs=pl.BlockSpec((PROJECT_BLOCKS, 16, BLK), lambda i: (i, 0, 0)),
        scratch_shapes=[
            pltpu.VMEM((PROJECT_BLOCKS, 16, BLK), f32),
            pltpu.VMEM((8, BLK), f32),
            pltpu.VMEM((3, 24, BLK), f32),
        ],
        compiler_params=params_of(PROJECT_MB),
        name="project",
    )(view_pose, gauss_params)


def update(gauss_params, first_moment, second_moment, own, after, low, high, prior):
    f32 = jnp.float32
    views = 4
    chunk = 8 * BLK
    return pl.pallas_call(
        update_kernel,
        out_shape=[jax.ShapeDtypeStruct(gauss_params.shape, f32)] * 3,
        in_specs=[VMEM] * 8,
        out_specs=[pl.BlockSpec(memory_space=pl.ANY)] * 3,
        scratch_shapes=[
            pltpu.VMEM((views, *own.shape), f32),
            pltpu.VMEM((8, 16, BLK), f32),
            pltpu.VMEM((8, 16, BLK), f32),
            pltpu.VMEM((views, 64, BLK), f32),
            pltpu.VMEM((2, 3, PARAMS, chunk), f32),
            pltpu.SemaphoreType.DMA((2, 3)),
        ],
        compiler_params=params_of(UPDATE_MB),
        name="update",
    )(gauss_params, first_moment, second_moment, own, after, low, high, prior)


def shards(
    gauss_params, first_moment, second_moment, view_pose, tile_blocks, tile_order, target_image
):
    groups = lax.axis_size("gs")
    views = lax.axis_size("view")
    columns = gauss_params.shape[1]
    blocks = columns // BLK
    tiles, slots = tile_blocks.shape[1:]
    f32, i32 = jnp.float32, jnp.int32
    shape = jax.ShapeDtypeStruct

    wanted, table, count = pl.pallas_call(
        request_kernel,
        out_shape=[shape((groups, 1, CAP), i32)] + [shape((1, tiles * slots), i32)] * 2,
        in_specs=[VMEM, VMEM],
        out_specs=[VMEM, VMEM, VMEM],
        name="requests",
    )(tile_blocks[0], tile_order[0])
    asked = lax.all_to_all(wanted, "gs", split_axis=0, concat_axis=0, tiled=True)
    feats = project(view_pose, gauss_params)
    outgoing = pl.pallas_call(
        pick_kernel,
        out_shape=shape((groups, FEATS, CAP, BLK), f32),
        in_specs=[SMEM, VMEM],
        out_specs=VMEM,
        compiler_params=params_of(16),
        name="pick",
    )(asked, feats)
    arrived = lax.all_to_all(outgoing, "gs", split_axis=0, concat_axis=0, tiled=True)
    image, back = render(table, count, arrived, jnp.transpose(target_image[0], (1, 0, 2)))
    landed = lax.all_to_all(back, "gs", split_axis=0, concat_axis=0, tiled=True)
    own = pl.pallas_call(
        land_kernel,
        out_shape=shape((blocks // (8 * HALF), FEATS * HALF + 1, 8, BLK), f32),
        in_specs=[SMEM, SMEM, VMEM, VMEM],
        out_specs=VMEM,
        scratch_shapes=[pltpu.VMEM((blocks + 1, 16, BLK), f32)],
        compiler_params=params_of(16),
        name="land",
    )(asked, view_pose, landed, feats)

    def from_next(value, k):
        return lax.ppermute(value, "view", [((i + k) % views, i) for i in range(views)])

    after = from_next(own, 1)
    prior = from_next(own, views - 1)
    low = from_next(after[:1], 1)
    high = from_next(prior[1:], views - 1)
    new_params, new_first, new_second = update(
        gauss_params, first_moment, second_moment, own, after, low, high, prior
    )
    return (new_params, new_first, new_second, jnp.transpose(image, (1, 0, 2))[None])


def solution(mesh):
    placed = (
        P(None, "gs"),
        P(None, "gs"),
        P(None, "gs"),
        P("view", None),
        P("view", "gs", None),
        P("view", "gs", None),
        P("view", "gs", None, None),
    )
    return jax.shard_map(
        shards,
        mesh=mesh,
        in_specs=placed,
        out_specs=(P(None, "gs"), P(None, "gs"), P(None, "gs"), P("view", "gs", None, None)),
        check_vma=False,
    )
```
